256 devices in a mesh: ctx: 32 (over x_lo, z, core), head: 8 (over y, x_hi).
Axes of the slice: x: 4 (x_hi: 2, x_lo: 2; x = x_hi * 2 + x_lo), y: 4, z: 8, core: 2. Of those that a mesh axis runs over, the one named last changes fastest.
Arguments:
- query_latent: bfloat16 [4096, 128, 512], P('ctx', 'head'), may hold values from -64 to 64
- query_rope: bfloat16 [4096, 8192], P('ctx', 'head'), may hold values from -3 to 3
- latent: bfloat16 [4096, 512], P('ctx'), may hold values from -4 to 4
- rope_key: bfloat16 [64, 4096], P(None, 'ctx'), may hold values from -5 to 5
- out_grad: bfloat16 [4096, 128, 512], P('ctx', 'head'), may hold values from -0.59765625 to 0.59765625
- doc_lengths: int32 [16], replicated, may hold values from 1 to 512, 4096 in all
Outputs:
- query_grad: bfloat16 [4096, 128, 512], P('ctx', 'head')
- query_rope_grad: bfloat16 [4096, 8192], P('ctx', 'head')
- latent_grad: bfloat16 [4096, 512], P('ctx')
- rope_key_grad: bfloat16 [64, 4096], P(None, 'ctx')
The draws below stay inside these ranges and needn't reach their ends.
Inputs may be any that keep to these rules, and one draw needn't show every extreme that they name: `doc_lengths`: the lengths sum to 4096; the longest document is exactly 512 positions long.
All inputs are finite; a program needn't handle non-finite values.
Results may differ from the reference program's by a relative error of at most 0.0083.
Values may be sent and summed in bfloat16 or wider, within the bound.
A program may use at most 64 MiB of HBM per device.

```python
import math
import jax
import jax.numpy as jnp
import numpy as np
from jax import lax

HEADS = 128
LATENT = 512
ROPE = 64
TOK_DEV = 128
SPAN = 4
TOKENS = 4096
MAXDOC = 512
DOCS = 16
N_CTX = 32


def shared_latent(key):
    return jnp.clip(jax.random.normal(key, (TOKENS, LATENT), jnp.float32), -4.0, 4.0)


def draw_latent(key, part):
    base = shared_latent(key)
    return base.astype(jnp.bfloat16)


def draw_query_latent(key, part):
    key = jax.random.fold_in(key, 2)
    noise_key = jax.random.fold_in(key, 0)
    query = 0.5 * jnp.clip(jax.random.normal(noise_key, (TOKENS, HEADS, LATENT), jnp.float32), -6.0, 6.0)
    return query.astype(jnp.bfloat16)


def block_levels(rng, shape, shards, least, high):
    factor_of, own = 1.0, jax.random.fold_in(rng, 6)
    for dim, parts in shards:
        draws = jnp.exp(jax.random.uniform(jax.random.fold_in(own, dim), (parts,), jnp.float32, least / len(shards), high / len(shards)))
        factor_of = factor_of * jnp.repeat(draws, shape[dim] // parts).reshape([-1 if axis == dim else 1 for axis in range(len(shape))])
    return factor_of


def profile(amount, total, most, skew):
    portions = [(1 << 20) // math.isqrt(grade ** skew) + 1 for grade in range(2, amount + 1)]
    spare, counts = total - most - (amount - 1), [1] * (amount - 1)
    while spare > 0:
        candidates = [i for i in range(amount - 1) if counts[i] < most]
        whole, remaining = sum([portions[i] for i in candidates]), spare
        for i in candidates:
            more = min(most - counts[i], max(1, remaining * portions[i] // whole), spare)
            counts[i] = counts[i] + more
            spare = spare - more
    return np.array([most] + counts)


def uneven(rng, amount, total, most, skew):
    if amount == 2:
        one = jax.random.randint(rng, (), max(1, total - most), min(most, total - 1) + 1)
        return jnp.stack([one, total - one])
    sizes = jnp.asarray(profile(amount, total, most, skew), jnp.int32)
    pairs = (amount - 1) // 2
    source_of, receiver = sizes[1:1 + 2 * pairs:2], sizes[2:2 + 2 * pairs:2]
    margin = jnp.minimum(source_of - 1, most - receiver)
    shifted = jax.random.randint(jax.random.fold_in(rng, 1), (pairs,), 0, 1 << 20) % (margin + 1)
    sizes = sizes.at[1:1 + 2 * pairs:2].set(source_of - shifted).at[2:2 + 2 * pairs:2].set(receiver + shifted)
    return sizes[jax.random.permutation(jax.random.fold_in(rng, 2), amount)]


def scatter_about(stream_key, extent, scale, limit, pieces=(), kind=jnp.bfloat16):
    values = scale * jax.random.normal(stream_key, extent, jnp.float32)
    if pieces:
        values = values * block_levels(stream_key, extent, pieces, -0.22, 0.18)
    return jnp.clip(values, -limit, limit).astype(kind)


def setup_inputs(seed: int = 0) -> dict:
    streams_of = jax.random.split(jax.random.key(seed), 7)
    query_latent = draw_query_latent(jax.random.fold_in(streams_of[6], 71), 0)
    query_rope = scatter_about(streams_of[1], (TOKENS, HEADS * ROPE), 0.5, 3.0, ((0, 32), (1, 8)))
    latent = draw_latent(jax.random.fold_in(streams_of[6], 71), 0)
    rope_key = scatter_about(streams_of[3], (ROPE, TOKENS), 1.0, 5.0, ((1, 32),))
    out_grad = scatter_about(streams_of[4], (TOKENS, HEADS, LATENT), 0.1, 0.59765625, ((0, 32), (1, 8)))
    doc_lengths = uneven(streams_of[5], DOCS, TOKENS, MAXDOC, 2).astype(jnp.int32)
    return dict(query_latent=query_latent, query_rope=query_rope, latent=latent, rope_key=rope_key, out_grad=out_grad, doc_lengths=doc_lengths)


softmax_scale = 192.0 ** -0.5


def doc_index(positions, doc_ends):
    return jnp.sum((positions[:, None] >= doc_ends[None, :]).astype(jnp.int32), axis=1)


def reference(query_latent, query_rope, latent, rope_key, out_grad, doc_lengths):
    window = (SPAN + 1) * TOK_DEV
    lead = SPAN * TOK_DEV
    doc_ends = jnp.cumsum(doc_lengths).astype(jnp.int32)
    padded_latent = jnp.concatenate([jnp.zeros((lead, LATENT), latent.dtype), latent], axis=0)
    padded_rope = jnp.concatenate([jnp.zeros((ROPE, lead), rope_key.dtype), rope_key], axis=1)
    rope_queries = query_rope.reshape(TOKENS, HEADS, ROPE)
    offsets = jnp.arange(TOK_DEV, dtype=jnp.int32)
    key_offsets = jnp.arange(window, dtype=jnp.int32)

    def step(carried, block_id):
        grad_latent, grad_rope = carried
        first_row = (block_id * TOK_DEV).astype(jnp.int32)
        q_lat = lax.dynamic_slice_in_dim(query_latent, first_row, TOK_DEV, 0).astype(jnp.float32)
        q_rope = lax.dynamic_slice_in_dim(rope_queries, first_row, TOK_DEV, 0).astype(jnp.float32)
        d_out = lax.dynamic_slice_in_dim(out_grad, first_row, TOK_DEV, 0).astype(jnp.float32)
        key_lat = lax.dynamic_slice_in_dim(padded_latent, first_row, window, 0).astype(jnp.float32)
        key_rope = lax.dynamic_slice_in_dim(padded_rope, first_row, window, 1).astype(jnp.float32)
        query_pos = first_row + offsets
        key_pos = first_row - lead + key_offsets
        allowed = (key_pos[None, :] >= 0) & (key_pos[None, :] <= query_pos[:, None])
        allowed = allowed & (doc_index(key_pos, doc_ends)[None, :] == doc_index(query_pos, doc_ends)[:, None])
        scores = jnp.einsum("thc,kc->thk", q_lat, key_lat) + jnp.einsum("thr,rk->thk", q_rope, key_rope)
        scores = jnp.where(allowed[:, None, :], scores * softmax_scale, -jnp.inf)
        row_max = jnp.max(scores, axis=-1, keepdims=True)
        weights_exp = jnp.exp(scores - row_max)
        probs = weights_exp / jnp.sum(weights_exp, axis=-1, keepdims=True)
        probs_b = lax.optimization_barrier(probs.astype(jnp.bfloat16)).astype(jnp.float32)
        attn_out = jnp.einsum("thk,kc->thc", probs_b, key_lat)
        row_delta = jnp.sum(d_out * attn_out, axis=-1)
        prob_grad = jnp.einsum("thc,kc->thk", d_out, key_lat)
        score_grad = (probs * (prob_grad - row_delta[:, :, None]) * softmax_scale).astype(jnp.bfloat16)
        score_grad = lax.optimization_barrier(score_grad).astype(jnp.float32)
        q_grad = jnp.einsum("thk,kc->thc", score_grad, key_lat).astype(jnp.bfloat16)
        qr_grad = jnp.einsum("thk,rk->thr", score_grad, key_rope).astype(jnp.bfloat16)
        lat_term = jnp.einsum("thk,thc->kc", probs_b, d_out) + jnp.einsum("thk,thc->kc", score_grad, q_lat)
        rope_term = jnp.einsum("thk,thr->rk", score_grad, q_rope)
        old_lat = lax.dynamic_slice_in_dim(grad_latent, first_row, window, 0)
        grad_latent = lax.dynamic_update_slice_in_dim(grad_latent, old_lat + lat_term, first_row, 0)
        old_rope = lax.dynamic_slice_in_dim(grad_rope, first_row, window, 1)
        grad_rope = lax.dynamic_update_slice_in_dim(grad_rope, old_rope + rope_term, first_row, 1)
        return (grad_latent, grad_rope), (q_grad, qr_grad)

    start_state = (jnp.zeros((lead + TOKENS, LATENT), jnp.float32), jnp.zeros((ROPE, lead + TOKENS), jnp.float32))
    final_state, outputs = lax.scan(step, start_state, jnp.arange(N_CTX, dtype=jnp.int32))
    query_grad = outputs[0].reshape(TOKENS, HEADS, LATENT)
    query_rope_grad = outputs[1].reshape(TOKENS, HEADS * ROPE)
    latent_grad = final_state[0][lead:].astype(jnp.bfloat16)
    rope_key_grad = final_state[1][:, lead:].astype(jnp.bfloat16)
    return query_grad, query_rope_grad, latent_grad, rope_key_grad
```

```python
import functools
import math

import jax
import jax.numpy as jnp
from jax import lax
from jax.experimental import pallas as pl
from jax.experimental.pallas import tpu as pltpu
from jax.sharding import PartitionSpec as P

MESH = pl.DeviceIdType.MESH
SPAN = 4
SLOTS = SPAN + 1
QUARTERS = 4
LANES = 128
TILE = 256
softmax_scale = 192.0 ** (-0.5)
exp2_scale = softmax_scale * math.log2(math.e)
f32 = jnp.float32
bf16 = jnp.bfloat16


def kernel(
    n_ctx,
    heads,
    len_ref,
    q_hbm,
    do_hbm,
    qr_ref,
    lat_ref,
    rope_ref,
    dq_hbm,
    dqr_ref,
    dlat_ref,
    drope_ref,
    q_v,
    do_v,
    q_t,
    do_t,
    qr_f,
    qr_v,
    s_v,
    dp_v,
    p_t,
    ds_t,
    dq_v,
    kbuf,
    kcat,
    k_t,
    gbuf,
    r1,
    s2,
    r2,
    v3,
    s3,
    r3,
    s4,
    r4,
    obuf,
    in_sem,
    out_sem,
    zs,
    zr,
    y1s,
    y1r,
    y2s,
    y2r,
    cs,
    cr,
    a1s,
    a1r,
    a2s,
    a2r,
    a3s,
    a3r,
    a4s,
    a4r,
    fxs,
    fxr,
    f1s,
    f1r,
    f2s,
    f2r,
):
    rows, width = q_v.shape
    tok = lat_ref.shape[0]
    rope = rope_ref.shape[0]
    tiles = rows // TILE
    krows = kbuf.shape[2]
    part = r3.shape[1]
    rest = krows - part

    ctx = lax.axis_index("ctx")
    head = lax.axis_index("head")
    core = ctx % 2
    y = head // 2
    xh = head % 2
    y_a = y + 1 - 2 * (y % 2)
    y_b = 3 - y
    y_opp = (y + 2) % 4
    y_p1 = y_a * (1 - core) + y_b * core
    y_p2 = y_b * (1 - core) + y_a * core
    here = (ctx, head)
    p1 = (ctx, y_p1 * 2 + xh)
    p2 = (ctx, y_p2 * 2 + xh)
    px = (ctx, y * 2 + 1 - xh)
    sib = (ctx + 1 - 2 * core, head)

    def along(by):
        return ((ctx + by + n_ctx) % n_ctx, head)

    def remote(src, dst, send, recv, to):
        return pltpu.make_async_remote_copy(
            src_ref=src, dst_ref=dst, send_sem=send, recv_sem=recv, device_id=to, device_id_type=MESH
        )

    in_q = pltpu.make_async_copy(q_hbm, q_v, in_sem.at[0])
    in_do = pltpu.make_async_copy(do_hbm, do_v, in_sem.at[1])
    in_q.start()
    in_do.start()

    barrier = pltpu.get_barrier_semaphore()
    peers = [p1, p2, px] + [along(by) for by in (-4, -3, -2, -1, 1, 2, 3, 4)]
    for peer in peers:
        pl.semaphore_signal(barrier, inc=1, device_id=peer, device_id_type=MESH)

    def own_keys():
        for q in range(QUARTERS):
            kbuf[0, q, :tok, :] = lat_ref[:, q * LANES : (q + 1) * LANES]
            kbuf[0, q, tok:, :] = rope_ref[q * 16 : (q + 1) * 16, :]

    own_keys()
    pl.semaphore_wait(barrier, len(peers))

    def z_copy(n):
        slot = 2 + 2 * n
        return remote(kbuf.at[0, y], kbuf.at[slot, y], zs.at[n], zr.at[n], along(slot))

    def y1_copy(n):
        slot = 2 + 2 * n
        return remote(kbuf.at[slot, y], kbuf.at[slot, y], y1s.at[n], y1r.at[n], p1)

    def y2_copy(n, k):
        slot = 2 + 2 * n
        quarter = (y, y_p1)[k]
        return remote(
            kbuf.at[slot, quarter], kbuf.at[slot, quarter], y2s.at[n, k], y2r.at[n, k], p2
        )

    def core_copy(src, n):
        return remote(kbuf.at[src], kbuf.at[1 + 2 * n], cs.at[n], cr.at[n], sib)

    z_copy(0).start()
    z_copy(1).start()

    @pl.when(core == 0)
    def _():
        core_copy(0, 0).start()

    def after_z(n):
        z_copy(n).wait_recv()
        y1_copy(n).start()

    def after_y1(n):
        y1_copy(n).wait_recv()
        y2_copy(n, 0).start()
        y2_copy(n, 1).start()

    def after_y2(n):
        y2_copy(n, 0).wait_recv()
        y2_copy(n, 1).wait_recv()
        if n == 0:

            @pl.when(core == 0)
            def _():
                core_copy(2, 1).start()

            @pl.when(core == 1)
            def _():
                core_copy(2, 0).start()
        else:

            @pl.when(core == 1)
            def _():
                core_copy(4, 1).start()

    def unpack(slot):
        at = slot * tok
        wide = jnp.concatenate([kbuf[slot, q, :tok, :] for q in range(QUARTERS)], axis=1)
        turned = jnp.concatenate([kbuf[slot, q, tok:, :] for q in range(QUARTERS)], axis=0)
        kcat[at : at + tok, :width] = wide
        padded = jnp.concatenate([turned, jnp.zeros((LANES - rope, tok), bf16)], axis=0)
        kcat[at : at + tok, width:] = padded.T
        k_t[:width, at : at + tok] = wide.T
        k_t[width:, at : at + tok] = turned

    def lanes(i):
        return pl.ds(pl.multiple_of(i * TILE, TILE), TILE)

    def turn_q(i, c):
        q_t[:width, lanes(i)] = q_v[lanes(i), :].T
        return c

    def turn_do(i, c):
        do_t[:, lanes(i)] = do_v[lanes(i), :].T
        return c

    def turn_rope(i, c):
        block = qr_f[lanes(i), :].astype(bf16)
        qr_v[lanes(i), :] = block
        q_t[width:, lanes(i)] = block.T
        return c

    def scores(first, count):
        def body(i, c):
            at = first * tok
            keys = kcat[at : at + count * tok, :]
            s_v[at : at + count * tok, lanes(i)] = jnp.dot(
                keys, q_t[:, lanes(i)], preferred_element_type=f32
            )
            dp_v[at : at + count * tok, lanes(i)] = jnp.dot(
                keys[:, :width], do_t[:, lanes(i)], preferred_element_type=f32
            )
            return c

        lax.fori_loop(0, tiles, body, 0)

    in_q.wait()
    lax.fori_loop(0, tiles, turn_q, 0)
    qr_f[...] = jnp.zeros_like(qr_f)
    for h in range(heads):
        qr_f[pl.ds(h, tok, stride=heads), :rope] = qr_ref[:, h * rope : (h + 1) * rope].astype(f32)
    lax.fori_loop(0, tiles, turn_rope, 0)
    after_z(0)
    unpack(0)
    in_do.wait()
    lax.fori_loop(0, tiles, turn_do, 0)
    after_y1(0)
    after_z(1)
    scores(0, 1)
    after_y2(0)
    after_y1(1)
    unpack(2)
    after_y2(1)
    core_copy(0, 0).wait_recv()
    unpack(1)
    scores(1, 2)
    unpack(4)
    core_copy(0, 1).wait_recv()
    unpack(3)
    scores(3, 2)

    ends = []
    total = jnp.int32(0)
    for k in range(len_ref.shape[0]):
        total = total + len_ref[k]
        ends.append(total - ctx * tok)

    def softmax(i, c):
        sl = lanes(i)
        token = (lax.broadcasted_iota(jnp.int32, (1, TILE), 1) + i * TILE) // heads
        low = jnp.full((1, TILE), -ctx * tok, jnp.int32)
        for end in ends:
            low = jnp.maximum(low, jnp.where(end <= token, end, low))
        key = lax.broadcasted_iota(jnp.int32, (tok, TILE), 0)
        top = jnp.full((1, TILE), -jnp.inf, f32)
        for d in range(SLOTS):
            at = pl.ds(d * tok, tok)
            ok = key >= low + d * tok
            if d == 0:
                ok = ok & (key <= token)
            s = jnp.where(ok, s_v[at, sl], -jnp.inf)
            s_v[at, sl] = s
            top = jnp.maximum(top, jnp.max(s, axis=0, keepdims=True))
        norm = jnp.zeros((1, TILE), f32)
        for d in range(SLOTS):
            at = pl.ds(d * tok, tok)
            e = jnp.exp2((s_v[at, sl] - top) * exp2_scale)
            s_v[at, sl] = e
            norm = norm + jnp.sum(e, axis=0, keepdims=True)
        inverse = 1.0 / norm
        delta = jnp.zeros((1, TILE), f32)
        for d in range(SLOTS):
            at = pl.ds(d * tok, tok)
            pb = (s_v[at, sl] * inverse).astype(bf16)
            p_t[at, sl] = pb
            delta = delta + jnp.sum(pb.astype(f32) * dp_v[at, sl], axis=0, keepdims=True)
        scaled = inverse * softmax_scale
        for d in range(SLOTS):
            at = pl.ds(d * tok, tok)
            ds_t[at, sl] = (s_v[at, sl] * scaled * (dp_v[at, sl] - delta)).astype(bf16)
        return c

    lax.fori_loop(0, tiles, softmax, 0)

    def key_terms(first, count):
        at = pl.ds(first * tok, count * tok)
        g = jnp.dot(p_t[at, :], do_v[...], preferred_element_type=f32)
        g = g + jnp.dot(ds_t[at, :], q_v[...], preferred_element_type=f32)
        gr = jnp.dot(ds_t[at, :], qr_v[...], preferred_element_type=f32)
        for k in range(count):
            piece = slice(k * tok, (k + 1) * tok)
            turned = gr[piece, :].T
            for q in range(QUARTERS):
                gbuf[first + k, q, :tok, :] = g[piece, q * LANES : (q + 1) * LANES].astype(bf16)
                gbuf[first + k, q, tok:, :] = turned[q * 16 : (q + 1) * 16, :].astype(bf16)

    def a1_copy(d, k):
        return remote(gbuf.at[d, (y_p1, y_opp)[k]], r1.at[d, k], a1s.at[d, k], a1r.at[d, k], p1)

    def a2_copy(d):
        return remote(s2.at[d], r2.at[d], a2s.at[d], a2r.at[d], p2)

    def a3_copy(d):
        away = pl.ds(pl.multiple_of(rest * (1 - xh), 16), part)
        return remote(s3.at[d, away], r3.at[d], a3s.at[d], a3r.at[d], px)

    def a4_copy(d):
        return remote(s4.at[d], r4.at[d], a4s.at[d], a4r.at[d], along(-d))

    def red1(d):
        a1_copy(d, 1).start()
        a1_copy(d, 0).start()

    def red2(d):
        a1_copy(d, 1).wait_recv()
        s2[d] = (gbuf[d, y_p2].astype(f32) + r1[d, 1].astype(f32)).astype(bf16)
        a2_copy(d).start()
        a1_copy(d, 0).wait_recv()

    def red3(d):
        mine = gbuf[d, y].astype(f32) + r1[d, 0].astype(f32)
        a2_copy(d).wait_recv()
        s3[d] = (mine + r2[d].astype(f32)).astype(bf16)
        a3_copy(d).start()

    near = pl.ds(pl.multiple_of(rest * xh, 16), part)

    def red4(d):
        a3_copy(d).wait_recv()
        both = s3[d, near].astype(f32) + r3[d].astype(f32)
        if d == 0:
            v3[...] = both
        else:
            s4[d] = both.astype(bf16)
            a4_copy(d).start()

    def fx_copy():
        whole = pl.ds(pl.multiple_of(part * xh, 16), rest)
        return remote(obuf.at[y, whole], obuf.at[y, whole], fxs, fxr, px)

    def fx_arrival():
        whole = pl.ds(pl.multiple_of(part * (1 - xh), 16), rest)
        return remote(obuf.at[y, whole], obuf.at[y, whole], fxs, fxr, px)

    def f1_copy():
        return remote(obuf.at[y], obuf.at[y], f1s, f1r, p1)

    def f2_copy(k):
        quarter = (y, y_p1)[k]
        return remote(obuf.at[quarter], obuf.at[quarter], f2s.at[k], f2r.at[k], p2)

    def out_copy(i):
        return pltpu.make_async_copy(dq_v.at[lanes(i)], dq_hbm.at[lanes(i)], out_sem.at[i])

    def query_terms(i, c):
        sl = lanes(i)
        turned = jnp.dot(k_t[...], ds_t[:, sl], preferred_element_type=f32)
        dq_v[sl, :] = turned[:width, :].astype(bf16).T
        qr_f[sl, :rope] = turned[width:, :].T
        out_copy(i).start()
        return c

    def query_run(first, last):
        lax.fori_loop(first, last, query_terms, 0)

    key_terms(3, 2)
    red1(4)
    red1(3)
    key_terms(1, 2)
    red1(2)
    red1(1)
    red2(4)
    red2(3)
    key_terms(0, 1)
    red1(0)
    red3(4)
    red3(3)
    red2(2)
    red2(1)
    quarter = tiles // 4
    query_run(0, quarter)
    red2(0)
    red4(4)
    red4(3)
    red3(2)
    red3(1)
    query_run(quarter, 2 * quarter)
    red3(0)
    red4(2)
    red4(1)
    query_run(2 * quarter, 3 * quarter)
    red4(0)
    query_run(3 * quarter, tiles)
    for h in range(heads):
        dqr_ref[:, h * rope : (h + 1) * rope] = qr_f[pl.ds(h, tok, stride=heads), :rope].astype(bf16)

    total_grad = v3[...]
    for d in range(1, SLOTS):
        a4_copy(d).wait_recv()
        total_grad = total_grad + r4[d].astype(f32)
    obuf[y, near] = total_grad.astype(bf16)
    fx_copy().start()
    fx_arrival().wait_recv()
    f1_copy().start()
    f1_copy().wait_recv()
    f2_copy(0).start()
    f2_copy(1).start()
    f2_copy(0).wait_recv()
    f2_copy(1).wait_recv()
    for q in range(QUARTERS):
        dlat_ref[:, q * LANES : (q + 1) * LANES] = obuf[q, :tok, :]
        drope_ref[q * 16 : (q + 1) * 16, :] = obuf[q, tok:, :]

    for i in range(tiles):
        out_copy(i).wait()
    for n in range(2):
        z_copy(n).wait_send()
        y1_copy(n).wait_send()
        y2_copy(n, 0).wait_send()
        y2_copy(n, 1).wait_send()
        core_copy(0, n).wait_send()
        f2_copy(n).wait_send()
    for d in range(SLOTS):
        a1_copy(d, 0).wait_send()
        a1_copy(d, 1).wait_send()
        a2_copy(d).wait_send()
        a3_copy(d).wait_send()
        if d:
            a4_copy(d).wait_send()
    fx_copy().wait_send()
    f1_copy().wait_send()


def local(query_latent, query_rope, latent, rope_key, out_grad, doc_lengths, n_ctx):
    tok, heads, width = query_latent.shape
    rope = rope_key.shape[0]
    rows = tok * heads
    keys = SLOTS * tok
    krows = tok + rope * tok // width
    half = (krows // 2 + 15) // 16 * 16
    dma = pltpu.SemaphoreType.DMA
    vmem = pltpu.VMEM
    in_vmem = pl.BlockSpec(memory_space=pltpu.VMEM)
    in_any = pl.BlockSpec(memory_space=pl.ANY)
    dq, dqr, dlat, drope = pl.pallas_call(
        functools.partial(kernel, n_ctx, heads),
        out_shape=(
            jax.ShapeDtypeStruct((rows, width), bf16),
            jax.ShapeDtypeStruct((tok, heads * rope), bf16),
            jax.ShapeDtypeStruct((tok, width), bf16),
            jax.ShapeDtypeStruct((rope, tok), bf16),
        ),
        in_specs=[pl.BlockSpec(memory_space=pltpu.SMEM), in_any, in_any, in_vmem, in_vmem, in_vmem],
        out_specs=(in_any, in_vmem, in_vmem, in_vmem),
        scratch_shapes=[
            vmem((rows, width), bf16),
            vmem((rows, width), bf16),
            vmem((width + LANES, rows), bf16),
            vmem((width, rows), bf16),
            vmem((rows, LANES), f32),
            vmem((rows, LANES), bf16),
            vmem((keys, rows), f32),
            vmem((keys, rows), f32),
            vmem((keys, rows), bf16),
            vmem((keys, rows), bf16),
            vmem((rows, width), bf16),
            vmem((SLOTS, QUARTERS, krows, LANES), bf16),
            vmem((keys, width + LANES), bf16),
            vmem((width + rope, keys), bf16),
            vmem((SLOTS, QUARTERS, krows, LANES), bf16),
            vmem((SLOTS, 2, krows, LANES), bf16),
            vmem((SLOTS, krows, LANES), bf16),
            vmem((SLOTS, krows, LANES), bf16),
            vmem((half, LANES), f32),
            vmem((SLOTS, krows, LANES), bf16),
            vmem((SLOTS, half, LANES), bf16),
            vmem((SLOTS, half, LANES), bf16),
            vmem((SLOTS, half, LANES), bf16),
            vmem((QUARTERS, krows, LANES), bf16),
            dma((2,)),
            dma((rows // TILE,)),
            dma((2,)),
            dma((2,)),
            dma((2,)),
            dma((2,)),
            dma((2, 2)),
            dma((2, 2)),
            dma((2,)),
            dma((2,)),
            dma((SLOTS, 2)),
            dma((SLOTS, 2)),
            dma((SLOTS,)),
            dma((SLOTS,)),
            dma((SLOTS,)),
            dma((SLOTS,)),
            dma((SLOTS,)),
            dma((SLOTS,)),
            dma,
            dma,
            dma,
            dma,
            dma((2,)),
            dma((2,)),
        ],
        compiler_params=pltpu.CompilerParams(
            collective_id=0, has_side_effects=True, vmem_limit_bytes=56 * 1024 * 1024
        ),
    )(
        doc_lengths,
        query_latent.reshape(rows, width),
        out_grad.reshape(rows, width),
        query_rope,
        latent,
        rope_key,
    )
    return dq.reshape(tok, heads, width), dqr, dlat, drope


def solution(mesh):
    in_specs = (
        P("ctx", "head", None),
        P("ctx", "head"),
        P("ctx", None),
        P(None, "ctx"),
        P("ctx", "head", None),
        P(),
    )
    out_specs = (P("ctx", "head", None), P("ctx", "head"), P("ctx", None), P(None, "ctx"))
    return jax.shard_map(
        functools.partial(local, n_ctx=mesh.shape["ctx"]),
        mesh=mesh,
        in_specs=in_specs,
        out_specs=out_specs,
        check_vma=False,
    )
```

```python
import functools
import math

import jax
import jax.numpy as jnp
from jax import lax
from jax.experimental import pallas as pl
from jax.experimental.pallas import tpu as pltpu
from jax.sharding import PartitionSpec as P

MESH = pl.DeviceIdType.MESH
SPAN = 4
SLOTS = SPAN + 1
BLOCKS = SPAN + 2
QUARTERS = 4
LANES = 128
TILE = 256
softmax_scale = 192.0 ** (-0.5)
exp2_scale = softmax_scale * math.log2(math.e)
f32 = jnp.float32
bf16 = jnp.bfloat16


def kernel(
    n_ctx,
    heads,
    len_ref,
    q_hbm,
    do_hbm,
    qr_ref,
    lat_ref,
    rope_ref,
    dq_hbm,
    dqr_ref,
    dlat_ref,
    drope_ref,
    q_v,
    do_v,
    q_t,
    do_t,
    qr_f,
    qr_v,
    low_v,
    top_v,
    norm_v,
    s_v,
    dp_v,
    p_t,
    ds_t,
    dq_v,
    kbuf,
    kcat,
    k_t,
    gbuf,
    rc,
    s1,
    ry,
    sz,
    rz,
    sx,
    rx,
    fo,
    obuf,
    in_sem,
    out_sem,
    zs,
    zr,
    ys,
    yr,
    cs,
    cr,
    bs,
    br,
    a1s,
    a1r,
    a2s,
    a2r,
    a3s,
    a3r,
    fs,
    fr,
):
    rows, width = q_v.shape
    tok = lat_ref.shape[0]
    rope = rope_ref.shape[0]
    tiles = rows // TILE
    krows = kbuf.shape[2]
    part = rz.shape[1]
    rest = krows - part

    ctx = lax.axis_index("ctx")
    head = lax.axis_index("head")
    core = ctx % 2
    y = head // 2
    xh = head % 2
    sib = ctx + 1 - 2 * core

    def other_y(k):
        return (y + k) % 4

    def along(by):
        return ((ctx + by + n_ctx) % n_ctx, head)

    def at_y(k, c=None):
        return (ctx if c is None else c, other_y(k) * 2 + xh)

    px = (ctx, y * 2 + 1 - xh)

    def remote(src, dst, send, recv, to):
        return pltpu.make_async_remote_copy(
            src_ref=src, dst_ref=dst, send_sem=send, recv_sem=recv, device_id=to, device_id_type=MESH
        )

    in_q = pltpu.make_async_copy(q_hbm, q_v, in_sem.at[0])
    in_do = pltpu.make_async_copy(do_hbm, do_v, in_sem.at[1])

    barrier = pltpu.get_barrier_semaphore()
    peers = [along(by) for by in (-4, -2, 2, 4)] + [px, (sib, head)]
    for k in (1, 2, 3):
        peers += [at_y(k), at_y(k, sib)]
    for peer in peers:
        pl.semaphore_signal(barrier, inc=1, device_id=peer, device_id_type=MESH)
    in_q.start()
    in_do.start()

    for q in range(QUARTERS):
        kbuf[0, q, :tok, :] = lat_ref[:, q * LANES : (q + 1) * LANES]
        kbuf[0, q, tok:, :] = rope_ref[q * 16 : (q + 1) * 16, :]
    unread = (BLOCKS - 1) * core
    gbuf[unread] = jnp.zeros(gbuf.shape[1:], bf16)
    pl.semaphore_wait(barrier, len(peers))

    def z4_copy():
        return remote(kbuf.at[0, y], kbuf.at[4, y], zs.at[1], zr.at[1], along(4))

    def z2_copy():
        return remote(kbuf.at[0], kbuf.at[2], zs.at[0], zr.at[0], along(2))

    def y_copy(k):
        return remote(kbuf.at[4, y], kbuf.at[4, y], ys.at[k - 1], yr.at[k - 1], at_y(k))

    def core_copy(src, n):
        return remote(kbuf.at[src], kbuf.at[1 + 2 * n], cs.at[n], cr.at[n], (sib, head))

    mine = pl.ds(pl.multiple_of(rest * core, 16), part)
    theirs = pl.ds(pl.multiple_of(rest * (1 - core), 16), part)

    def b_copy(d):
        b = d + 1 - core
        return remote(gbuf.at[b, :, theirs], rc.at[b], bs.at[b], br.at[b], (sib, head))

    def b_unread():
        return remote(
            gbuf.at[unread, :, theirs], rc.at[unread], bs.at[unread], br.at[unread], (sib, head)
        )

    def b_arrival(b):
        return remote(gbuf.at[b, :, theirs], rc.at[b], bs.at[b], br.at[b], (sib, head))

    z4_copy().start()
    z2_copy().start()

    @pl.when(core == 0)
    def _():
        core_copy(0, 0).start()

    b_unread().start()

    def after_z4():
        z4_copy().wait_recv()
        for k in (2, 1, 3):
            y_copy(k).start()

    def after_z2():
        z2_copy().wait_recv()

        @pl.when(core == 0)
        def _():
            core_copy(2, 1).start()

        @pl.when(core == 1)
        def _():
            core_copy(2, 0).start()

    def after_y():
        for k in (1, 2, 3):
            y_copy(k).wait_recv()

        @pl.when(core == 1)
        def _():
            core_copy(4, 1).start()

    def unpack(slot):
        at = slot * tok
        wide = jnp.concatenate([kbuf[slot, q, :tok, :] for q in range(QUARTERS)], axis=1)
        turned = jnp.concatenate([kbuf[slot, q, tok:, :] for q in range(QUARTERS)], axis=0)
        kcat[at : at + tok, :width] = wide
        padded = jnp.concatenate([turned, jnp.zeros((LANES - rope, tok), bf16)], axis=0)
        kcat[at : at + tok, width:] = padded.T
        k_t[:width, at : at + tok] = wide.T
        k_t[width:, at : at + tok] = turned

    def lanes(i):
        return pl.ds(pl.multiple_of(i * TILE, TILE), TILE)

    def token_of(i):
        return (lax.broadcasted_iota(jnp.int32, (1, TILE), 1) + i * TILE) // heads

    def turn_q(i, c):
        q_t[:width, lanes(i)] = q_v[lanes(i), :].T
        return c

    def turn_do(i, c):
        do_t[:, lanes(i)] = do_v[lanes(i), :].T
        return c

    def turn_rope(i, c):
        block = qr_f[lanes(i), :].astype(bf16)
        qr_v[lanes(i), :] = block
        q_t[width:, lanes(i)] = block.T
        return c

    ends = []
    total = jnp.int32(0)
    for k in range(len_ref.shape[0]):
        total = total + len_ref[k]
        ends.append(total - ctx * tok)

    def first_key(i, c):
        token = token_of(i)
        low = jnp.full((1, TILE), -ctx * tok, jnp.int32)
        for end in ends:
            low = jnp.maximum(low, jnp.where(end <= token, end, low))
        low_v[:, lanes(i)] = low
        return c

    def chunk(n, first, count, i):
        sl = lanes(i)
        at = pl.ds(first * tok, count * tok)
        keys = kcat[at, :]
        s = jnp.dot(keys, q_t[:, sl], preferred_element_type=f32)
        dp_v[at, sl] = jnp.dot(keys[:, :width], do_t[:, sl], preferred_element_type=f32)
        low = low_v[:, sl]
        key = lax.broadcasted_iota(jnp.int32, (tok, TILE), 0)
        masked = []
        for k in range(count):
            d = first + k
            ok = key >= low + d * tok
            if d == 0:
                ok = ok & (key <= token_of(i))
            masked.append(jnp.where(ok, s[k * tok : (k + 1) * tok], -jnp.inf))
        top = jnp.full((1, TILE), -1e30, f32)
        for m in masked:
            top = jnp.maximum(top, jnp.max(m, axis=0, keepdims=True))
        norm = jnp.zeros((1, TILE), f32)
        for k in range(count):
            e = jnp.exp2((masked[k] - top) * exp2_scale)
            s_v[pl.ds((first + k) * tok, tok), sl] = e
            norm = norm + jnp.sum(e, axis=0, keepdims=True)
        top_v[n : n + 1, sl] = top
        norm_v[n : n + 1, sl] = norm

    def finish(i):
        sl = lanes(i)
        tops = [top_v[n : n + 1, sl] for n in range(3)]
        top = jnp.maximum(jnp.maximum(tops[0], tops[1]), tops[2])
        shares = [jnp.exp2((t - top) * exp2_scale) for t in tops]
        norm = sum(shares[n] * norm_v[n : n + 1, sl] for n in range(3))
        inverse = 1.0 / norm
        weights = [share * inverse for share in shares]
        delta = jnp.zeros((1, TILE), f32)
        for d in range(SLOTS):
            at = pl.ds(d * tok, tok)
            pb = (s_v[at, sl] * weights[(d + 1) // 2]).astype(bf16)
            p_t[at, sl] = pb
            delta = delta + jnp.sum(pb.astype(f32) * dp_v[at, sl], axis=0, keepdims=True)
        for d in range(SLOTS):
            at = pl.ds(d * tok, tok)
            scaled = weights[(d + 1) // 2] * softmax_scale
            ds_t[at, sl] = (s_v[at, sl] * scaled * (dp_v[at, sl] - delta)).astype(bf16)

    def scores(n, first, count):
        def body(i, c):
            chunk(n, first, count, i)
            return c

        lax.fori_loop(0, tiles, body, 0)

    def last_scores():
        def body(i, c):
            chunk(2, 3, 2, i)
            finish(i)
            return c

        lax.fori_loop(0, tiles, body, 0)

    in_q.wait()
    lax.fori_loop(0, tiles, turn_q, 0)
    qr_f[...] = jnp.zeros_like(qr_f)
    for h in range(heads):
        qr_f[pl.ds(h, tok, stride=heads), :rope] = qr_ref[:, h * rope : (h + 1) * rope].astype(f32)
    lax.fori_loop(0, tiles, turn_rope, 0)
    lax.fori_loop(0, tiles, first_key, 0)
    unpack(0)
    in_do.wait()
    lax.fori_loop(0, tiles, turn_do, 0)
    after_z4()
    scores(0, 0, 1)
    after_z2()
    unpack(2)
    core_copy(0, 0).wait_recv()
    unpack(1)
    scores(1, 1, 2)
    after_y()
    unpack(4)
    core_copy(0, 1).wait_recv()
    unpack(3)
    last_scores()

    def key_terms(first, count):
        at = pl.ds(first * tok, count * tok)
        g = jnp.dot(p_t[at, :], do_v[...], preferred_element_type=f32)
        g = g + jnp.dot(ds_t[at, :], q_v[...], preferred_element_type=f32)
        gr = jnp.dot(ds_t[at, :], qr_v[...], preferred_element_type=f32)
        for k in range(count):
            b = first + k + 1 - core
            piece = slice(k * tok, (k + 1) * tok)
            turned = gr[piece, :].T
            for q in range(QUARTERS):
                gbuf[b, q, :tok, :] = g[piece, q * LANES : (q + 1) * LANES].astype(bf16)
                gbuf[b, q, tok:, :] = turned[q * 16 : (q + 1) * 16, :].astype(bf16)
        for k in range(count):
            b_copy(first + k).start()

    def a1_copy(b, k):
        return remote(
            s1.at[b, other_y(k)], ry.at[b, k - 1], a1s.at[b, k - 1], a1r.at[b, k - 1], at_y(k)
        )

    def a2_copy(n):
        return remote(sz.at[n], rz.at[n], a2s.at[n], a2r.at[n], along((-2, -4)[n // 2]))

    def a3_copy():
        return remote(sx, rx, a3s, a3r, px)

    def red1(b):
        b_arrival(b).wait_recv()
        for q in range(QUARTERS):
            s1[b, q] = (gbuf[b, q, mine].astype(f32) + rc[b, q].astype(f32)).astype(bf16)
        for k in (2, 1, 3):
            a1_copy(b, k).start()

    def red2(b):
        summed = s1[b, y].astype(f32)
        for k in (1, 2, 3):
            a1_copy(b, k).wait_recv()
            summed = summed + ry[b, k - 1].astype(f32)
        if b >= 2:
            sz[b - 2] = summed.astype(bf16)
            a2_copy(b - 2).start()
        return summed

    def f_copy(cross, k):
        block = core if cross else 1 - core
        return remote(
            fo.at[block],
            obuf.at[y, core],
            fs.at[cross, k],
            fr.at[cross, k],
            at_y(k, sib) if cross else at_y(k),
        )

    def out_copy(i):
        return pltpu.make_async_copy(dq_v.at[lanes(i)], dq_hbm.at[lanes(i)], out_sem.at[i])

    def query_terms(i, c):
        sl = lanes(i)
        turned = jnp.dot(k_t[...], ds_t[:, sl], preferred_element_type=f32)
        dq_v[sl, :] = turned[:width, :].astype(bf16).T
        qr_f[sl, :rope] = turned[width:, :].T
        out_copy(i).start()
        return c

    def query_run(first, last):
        lax.fori_loop(first, last, query_terms, 0)

    key_terms(3, 2)
    key_terms(1, 2)
    red1(5)
    red1(4)
    key_terms(0, 1)
    red1(3)
    red1(2)
    quarter = tiles // 4
    query_run(0, quarter)
    red1(1)
    red1(0)
    red2(5)
    red2(4)
    query_run(quarter, 2 * quarter)
    red2(3)
    red2(2)
    query_run(2 * quarter, 3 * quarter)
    sums = [red2(0), red2(1)]
    query_run(3 * quarter, tiles)
    for h in range(heads):
        dqr_ref[:, h * rope : (h + 1) * rope] = qr_f[pl.ds(h, tok, stride=heads), :rope].astype(bf16)

    for j in range(2):
        a2_copy(j).wait_recv()
        a2_copy(2 + j).wait_recv()
        sx[j] = (sums[j] + rz[j].astype(f32) + rz[2 + j].astype(f32)).astype(bf16)
    a3_copy().start()
    a3_copy().wait_recv()
    fo[...] = (sx[...].astype(f32) + rx[...].astype(f32)).astype(bf16)
    for k in (2, 1, 3):
        f_copy(0, k).start()
        f_copy(1, k).start()
    f_copy(1, 0).start()
    obuf[y, core] = fo[1 - core]
    for k in range(4):
        f_copy(1, k).wait_recv()
        if k:
            f_copy(0, k).wait_recv()
    for q in range(QUARTERS):
        sl = slice(q * LANES, (q + 1) * LANES)
        dlat_ref[:part, sl] = obuf[q, 0]
        dlat_ref[part:, sl] = obuf[q, 1, part - rest : tok - rest, :]
        drope_ref[q * 16 : (q + 1) * 16, :] = obuf[q, 1, tok - rest :, :]

    for i in range(tiles):
        out_copy(i).wait()
    z2_copy().wait_send()
    z4_copy().wait_send()
    for n in range(2):
        core_copy(0, n).wait_send()
    for b in range(BLOCKS):
        b_arrival(b).wait_send()
    for k in (1, 2, 3):
        y_copy(k).wait_send()
        f_copy(0, k).wait_send()
        for b in range(BLOCKS):
            a1_copy(b, k).wait_send()
    for n in range(4):
        a2_copy(n).wait_send()
        f_copy(1, n).wait_send()
    a3_copy().wait_send()


def settle(*refs):
    half = (len(refs) - 2) // 3
    sems = refs[-2:]
    copies = []
    for n in range(half):
        src, dst, room = refs[n], refs[half + n], refs[2 * half + n]
        pieces = 8 if n == 0 else 1
        step = src.shape[0] // pieces
        for p in range(pieces):
            at = pl.ds(p * step, step)
            k = len(copies)
            copies.append(
                (
                    pltpu.make_async_copy(src.at[at], room.at[at], sems[0].at[k]),
                    pltpu.make_async_copy(room.at[at], dst.at[at], sems[1].at[k]),
                )
            )
    for first, _ in copies:
        first.start()
    for first, second in copies:
        first.wait()
        second.start()
    for _, second in copies:
        second.wait()


def local(query_latent, query_rope, latent, rope_key, out_grad, doc_lengths, n_ctx):
    tok, heads, width = query_latent.shape
    rope = rope_key.shape[0]
    rows = tok * heads
    keys = SLOTS * tok
    krows = tok + rope * tok // width
    half = (krows // 2 + 15) // 16 * 16
    dma = pltpu.SemaphoreType.DMA
    vmem = pltpu.VMEM
    in_vmem = pl.BlockSpec(memory_space=pltpu.VMEM)
    in_any = pl.BlockSpec(memory_space=pl.ANY)
    shapes = (
        jax.ShapeDtypeStruct((rows, width), bf16),
        jax.ShapeDtypeStruct((tok, heads * rope), bf16),
        jax.ShapeDtypeStruct((tok, width), bf16),
        jax.ShapeDtypeStruct((rope, tok), bf16),
    )
    outs = pl.pallas_call(
        functools.partial(kernel, n_ctx, heads),
        out_shape=shapes,
        in_specs=[pl.BlockSpec(memory_space=pltpu.SMEM), in_any, in_any, in_vmem, in_vmem, in_vmem],
        out_specs=(in_any, in_vmem, in_vmem, in_vmem),
        scratch_shapes=[
            vmem((rows, width), bf16),
            vmem((rows, width), bf16),
            vmem((width + LANES, rows), bf16),
            vmem((width, rows), bf16),
            vmem((rows, LANES), f32),
            vmem((rows, LANES), bf16),
            vmem((1, rows), jnp.int32),
            vmem((8, rows), f32),
            vmem((8, rows), f32),
            vmem((keys, rows), f32),
            vmem((keys, rows), f32),
            vmem((keys, rows), bf16),
            vmem((keys, rows), bf16),
            vmem((rows, width), bf16),
            vmem((SLOTS, QUARTERS, krows, LANES), bf16),
            vmem((keys, width + LANES), bf16),
            vmem((width + rope, keys), bf16),
            vmem((BLOCKS, QUARTERS, krows, LANES), bf16),
            vmem((BLOCKS, QUARTERS, half, LANES), bf16),
            vmem((BLOCKS, QUARTERS, half, LANES), bf16),
            vmem((BLOCKS, 3, half, LANES), bf16),
            vmem((4, half, LANES), bf16),
            vmem((4, half, LANES), bf16),
            vmem((2, half, LANES), bf16),
            vmem((2, half, LANES), bf16),
            vmem((2, half, LANES), bf16),
            vmem((QUARTERS, 2, half, LANES), bf16),
            dma((2,)),
            dma((rows // TILE,)),
            dma((2,)),
            dma((2,)),
            dma((3,)),
            dma((3,)),
            dma((2,)),
            dma((2,)),
            dma((BLOCKS,)),
            dma((BLOCKS,)),
            dma((BLOCKS, 3)),
            dma((BLOCKS, 3)),
            dma((4,)),
            dma((4,)),
            dma,
            dma,
            dma((2, 4)),
            dma((2, 4)),
        ],
        compiler_params=pltpu.CompilerParams(
            collective_id=0, has_side_effects=True, vmem_limit_bytes=56 * 1024 * 1024
        ),
    )(
        doc_lengths,
        query_latent.reshape(rows, width),
        out_grad.reshape(rows, width),
        query_rope,
        latent,
        rope_key,
    )
    dq, dqr, dlat, drope = pl.pallas_call(
        settle,
        out_shape=shapes,
        in_specs=[in_any] * 4,
        out_specs=(in_any,) * 4,
        scratch_shapes=[vmem(x.shape, x.dtype) for x in shapes] + [dma((11,)), dma((11,))],
    )(*outs)
    return dq.reshape(tok, heads, width), dqr, dlat, drope


def solution(mesh):
    in_specs = (
        P("ctx", "head", None),
        P("ctx", "head"),
        P("ctx", None),
        P(None, "ctx"),
        P("ctx", "head", None),
        P(),
    )
    out_specs = (P("ctx", "head", None), P("ctx", "head"), P("ctx", None), P(None, "ctx"))
    return jax.shard_map(
        functools.partial(local, n_ctx=mesh.shape["ctx"]),
        mesh=mesh,
        in_specs=in_specs,
        out_specs=out_specs,
        check_vma=False,
    )
```

```python
import functools
import math

import jax
import jax.numpy as jnp
from jax import lax
from jax.experimental import pallas as pl
from jax.experimental.pallas import tpu as pltpu
from jax.sharding import PartitionSpec as P

MESH = pl.DeviceIdType.MESH
SPAN = 4
SLOTS = SPAN + 1
BLOCKS = SPAN + 2
QUARTERS = 4
LANES = 128
TILE = 512
softmax_scale = 192.0 ** (-0.5)
exp2_scale = softmax_scale * math.log2(math.e)
f32 = jnp.float32
bf16 = jnp.bfloat16


def kernel(
    n_ctx,
    heads,
    len_ref,
    q_hbm,
    do_hbm,
    qr_ref,
    lat_ref,
    rope_ref,
    dq_hbm,
    dqr_ref,
    dlat_ref,
    drope_ref,
    q_v,
    do_v,
    q_t,
    do_t,
    qr_f,
    qr_v,
    low_v,
    top_v,
    norm_v,
    s_v,
    dp_v,
    p_t,
    ds_t,
    dq_v,
    kbuf,
    kcat,
    k_t,
    gbuf,
    rc,
    s1,
    ry,
    sz,
    rz,
    sx,
    rx,
    fo,
    obuf,
    in_sem,
    out_sem,
    zs,
    zr,
    ys,
    yr,
    cs,
    cr,
    bs,
    br,
    a1s,
    a1r,
    a2s,
    a2r,
    a3s,
    a3r,
    fs,
    fr,
):
    rows, width = q_v.shape
    tok = lat_ref.shape[0]
    rope = rope_ref.shape[0]
    tiles = rows // TILE
    krows = kbuf.shape[2]
    part = rz.shape[2]
    rest = krows - part

    ctx = lax.axis_index("ctx")
    head = lax.axis_index("head")
    core = ctx % 2
    y = head // 2
    xh = head % 2
    sib = ctx + 1 - 2 * core

    def other_y(k):
        return (y + k) % 4

    def along(by):
        return ((ctx + by + n_ctx) % n_ctx, head)

    def at_y(k, c=None):
        return (ctx if c is None else c, other_y(k) * 2 + xh)

    px = (ctx, y * 2 + 1 - xh)

    def remote(src, dst, send, recv, to):
        return pltpu.make_async_remote_copy(
            src_ref=src, dst_ref=dst, send_sem=send, recv_sem=recv, device_id=to, device_id_type=MESH
        )

    in_q = pltpu.make_async_copy(q_hbm, q_v, in_sem.at[0])
    in_do = pltpu.make_async_copy(do_hbm, do_v, in_sem.at[1])

    barrier = pltpu.get_barrier_semaphore()
    peers = [along(by) for by in (-4, -2, 2, 4)] + [px, (sib, head)]
    for k in (1, 2, 3):
        peers += [at_y(k), at_y(k, sib)]
    for peer in peers:
        pl.semaphore_signal(barrier, inc=1, device_id=peer, device_id_type=MESH)
    in_q.start()
    in_do.start()

    for q in range(QUARTERS):
        kbuf[0, q, :tok, :] = lat_ref[:, q * LANES : (q + 1) * LANES]
        kbuf[0, q, tok:, :] = rope_ref[q * 16 : (q + 1) * 16, :]
    unread = (BLOCKS - 1) * core
    gbuf[unread] = jnp.zeros(gbuf.shape[1:], bf16)
    pl.semaphore_wait(barrier, len(peers))

    def z4_copy():
        return remote(kbuf.at[0, y], kbuf.at[4, y], zs.at[1], zr.at[1], along(4))

    def z2_copy():
        return remote(kbuf.at[0], kbuf.at[2], zs.at[0], zr.at[0], along(2))

    def y_copy(k):
        return remote(kbuf.at[4, y], kbuf.at[4, y], ys.at[k - 1], yr.at[k - 1], at_y(k))

    def core_copy(src, n):
        return remote(kbuf.at[src], kbuf.at[1 + 2 * n], cs.at[n], cr.at[n], (sib, head))

    mine = pl.ds(pl.multiple_of(rest * core, 16), part)
    theirs = pl.ds(pl.multiple_of(rest * (1 - core), 16), part)

    def b_copy(first, count):
        b = pl.ds(first + 1 - core, count)
        n = (first + 1) // 2
        return remote(gbuf.at[b, :, theirs], rc.at[b], bs.at[n], br.at[n], (sib, head))

    def b_unread():
        return remote(gbuf.at[unread, :, theirs], rc.at[unread], bs.at[3], br.at[3], (sib, head))

    z4_copy().start()
    z2_copy().start()

    @pl.when(core == 0)
    def _():
        core_copy(0, 0).start()

    b_unread().start()

    def after_z4():
        z4_copy().wait_recv()
        for k in (2, 1, 3):
            y_copy(k).start()

    def after_z2():
        z2_copy().wait_recv()

        @pl.when(core == 0)
        def _():
            core_copy(2, 1).start()

        @pl.when(core == 1)
        def _():
            core_copy(2, 0).start()

    def after_y():
        for k in (1, 2, 3):
            y_copy(k).wait_recv()

        @pl.when(core == 1)
        def _():
            core_copy(4, 1).start()

    def unpack(slot):
        at = slot * tok
        wide = jnp.concatenate([kbuf[slot, q, :tok, :] for q in range(QUARTERS)], axis=1)
        turned = jnp.concatenate([kbuf[slot, q, tok:, :] for q in range(QUARTERS)], axis=0)
        kcat[at : at + tok, :width] = wide
        padded = jnp.concatenate([turned, jnp.zeros((LANES - rope, tok), bf16)], axis=0)
        kcat[at : at + tok, width:] = padded.T
        k_t[:width, at : at + tok] = wide.T
        k_t[width:, at : at + tok] = turned

    def lanes(i):
        return pl.ds(pl.multiple_of(i * TILE, TILE), TILE)

    def token_of(i):
        return (lax.broadcasted_iota(jnp.int32, (1, TILE), 1) + i * TILE) // heads

    def turn_q(i, c):
        q_t[:width, lanes(i)] = q_v[lanes(i), :].T
        return c

    def turn_do(i, c):
        do_t[:, lanes(i)] = do_v[lanes(i), :].T
        return c

    def turn_rope(i, c):
        block = qr_f[lanes(i), :].astype(bf16)
        qr_v[lanes(i), :] = block
        q_t[width:, lanes(i)] = block.T
        return c

    ends = []
    total = jnp.int32(0)
    for k in range(len_ref.shape[0]):
        total = total + len_ref[k]
        ends.append(total - ctx * tok)

    def first_key(i, c):
        token = token_of(i)
        low = jnp.full((1, TILE), -ctx * tok, jnp.int32)
        for end in ends:
            low = jnp.maximum(low, jnp.where(end <= token, end, low))
        low_v[:, lanes(i)] = low
        return c

    def chunk(n, first, count, i):
        sl = lanes(i)
        at = pl.ds(first * tok, count * tok)
        keys = kcat[at, :]
        s = jnp.dot(keys, q_t[:, sl], preferred_element_type=f32)
        dp_v[at, sl] = jnp.dot(keys[:, :width], do_t[:, sl], preferred_element_type=f32)
        low = low_v[:, sl]
        key = lax.broadcasted_iota(jnp.int32, (tok, TILE), 0)
        masked = []
        for k in range(count):
            d = first + k
            ok = key >= low + d * tok
            if d == 0:
                ok = ok & (key <= token_of(i))
            masked.append(jnp.where(ok, s[k * tok : (k + 1) * tok], -jnp.inf))
        top = jnp.full((1, TILE), -1e30, f32)
        for m in masked:
            top = jnp.maximum(top, jnp.max(m, axis=0, keepdims=True))
        norm = jnp.zeros((1, TILE), f32)
        for k in range(count):
            e = jnp.exp2((masked[k] - top) * exp2_scale)
            s_v[pl.ds((first + k) * tok, tok), sl] = e
            norm = norm + jnp.sum(e, axis=0, keepdims=True)
        top_v[n : n + 1, sl] = top
        norm_v[n : n + 1, sl] = norm

    def finish(i):
        sl = lanes(i)
        tops = [top_v[n : n + 1, sl] for n in range(3)]
        top = jnp.maximum(jnp.maximum(tops[0], tops[1]), tops[2])
        shares = [jnp.exp2((t - top) * exp2_scale) for t in tops]
        norm = sum(shares[n] * norm_v[n : n + 1, sl] for n in range(3))
        inverse = 1.0 / norm
        weights = [share * inverse for share in shares]
        delta = jnp.zeros((1, TILE), f32)
        for d in range(SLOTS):
            at = pl.ds(d * tok, tok)
            pb = (s_v[at, sl] * weights[(d + 1) // 2]).astype(bf16)
            p_t[at, sl] = pb
            delta = delta + jnp.sum(pb.astype(f32) * dp_v[at, sl], axis=0, keepdims=True)
        for d in range(SLOTS):
            at = pl.ds(d * tok, tok)
            scaled = weights[(d + 1) // 2] * softmax_scale
            ds_t[at, sl] = (s_v[at, sl] * scaled * (dp_v[at, sl] - delta)).astype(bf16)

    def scores(n, first, count):
        def body(i, c):
            chunk(n, first, count, i)
            return c

        lax.fori_loop(0, tiles, body, 0, unroll=4)

    def last_scores():
        def body(i, c):
            chunk(2, 3, 2, i)
            finish(i)
            return c

        lax.fori_loop(0, tiles, body, 0, unroll=4)

    in_q.wait()
    lax.fori_loop(0, tiles, turn_q, 0, unroll=4)
    qr_f[...] = jnp.zeros_like(qr_f)
    for h in range(heads):
        qr_f[pl.ds(h, tok, stride=heads), :rope] = qr_ref[:, h * rope : (h + 1) * rope].astype(f32)
    lax.fori_loop(0, tiles, turn_rope, 0, unroll=4)
    lax.fori_loop(0, tiles, first_key, 0)
    unpack(0)
    in_do.wait()
    lax.fori_loop(0, tiles, turn_do, 0, unroll=4)
    after_z4()
    scores(0, 0, 1)
    after_z2()
    unpack(2)
    core_copy(0, 0).wait_recv()
    unpack(1)
    scores(1, 1, 2)
    after_y()
    unpack(4)
    core_copy(0, 1).wait_recv()
    unpack(3)
    last_scores()

    def key_dots(first, count):
        at = pl.ds(first * tok, count * tok)
        g = jnp.dot(p_t[at, :], do_v[...], preferred_element_type=f32)
        g = g + jnp.dot(ds_t[at, :], q_v[...], preferred_element_type=f32)
        gr = jnp.dot(ds_t[at, :], qr_v[...], preferred_element_type=f32)
        for k in range(count):
            b = first + k + 1 - core
            piece = slice(k * tok, (k + 1) * tok)
            turned = gr[piece, :].T
            for q in range(QUARTERS):
                gbuf[b, q, :tok, :] = g[piece, q * LANES : (q + 1) * LANES].astype(bf16)
                gbuf[b, q, tok:, :] = turned[q * 16 : (q + 1) * 16, :].astype(bf16)

    def key_terms(first, count):
        key_dots(first, count)
        b_copy(first, count).start()

    def a1_copy(pair, k):
        two = pl.ds(2 * pair, 2)
        return remote(
            s1.at[other_y(k), two],
            ry.at[k - 1, two],
            a1s.at[pair, k - 1],
            a1r.at[pair, k - 1],
            at_y(k),
        )

    def a2_copy(pair):
        n = pair - 1
        return remote(sz.at[n], rz.at[n], a2s.at[n], a2r.at[n], along(-2 * pair))

    def a3_copy():
        return remote(sx, rx, a3s, a3r, px)

    def red1(pair):
        if pair == 0:
            b_copy(0, 1).wait_recv()
        elif pair == 1:
            b_copy(1, 2).wait_recv()
        else:
            b_copy(3, 2).wait_recv()
            b_unread().wait_recv()
        for b in (2 * pair, 2 * pair + 1):
            for q in range(QUARTERS):
                s1[q, b] = (gbuf[b, q, mine].astype(f32) + rc[b, q].astype(f32)).astype(bf16)
        for k in (2, 1, 3):
            a1_copy(pair, k).start()

    def red2(pair):
        two = pl.ds(2 * pair, 2)
        summed = s1[y, two].astype(f32)
        for k in (1, 2, 3):
            a1_copy(pair, k).wait_recv()
            summed = summed + ry[k - 1, two].astype(f32)
        if pair:
            sz[pair - 1] = summed.astype(bf16)
            a2_copy(pair).start()
        return summed

    def f_copy(cross, k):
        block = core if cross else 1 - core
        return remote(
            fo.at[block],
            obuf.at[y, core],
            fs.at[cross, k],
            fr.at[cross, k],
            at_y(k, sib) if cross else at_y(k),
        )

    def out_copy(i):
        return pltpu.make_async_copy(dq_v.at[lanes(i)], dq_hbm.at[lanes(i)], out_sem.at[i])

    def query_terms(i, c):
        sl = lanes(i)
        turned = jnp.dot(k_t[...], ds_t[:, sl], preferred_element_type=f32)
        dq_v[sl, :] = turned[:width, :].astype(bf16).T
        qr_f[sl, :rope] = turned[width:, :].T
        out_copy(i).start()
        return c

    def query_run(first, last):
        lax.fori_loop(first, last, query_terms, 0)

    key_terms(3, 2)
    key_terms(1, 2)
    red1(2)
    key_terms(0, 1)
    red1(1)
    query_run(0, 1)
    red1(0)
    query_run(1, tiles // 2)
    red2(2)
    red2(1)
    own = red2(0)
    query_run(tiles // 2, tiles)
    for h in range(heads):
        dqr_ref[:, h * rope : (h + 1) * rope] = qr_f[pl.ds(h, tok, stride=heads), :rope].astype(bf16)

    a2_copy(2).wait_recv()
    a2_copy(1).wait_recv()
    sx[...] = (own + rz[0].astype(f32) + rz[1].astype(f32)).astype(bf16)
    a3_copy().start()
    a3_copy().wait_recv()
    fo[...] = (sx[...].astype(f32) + rx[...].astype(f32)).astype(bf16)
    for k in (2, 1, 3):
        f_copy(0, k).start()
        f_copy(1, k).start()
    f_copy(1, 0).start()
    obuf[y, core] = fo[1 - core]
    for k in range(4):
        f_copy(1, k).wait_recv()
        if k:
            f_copy(0, k).wait_recv()
    for q in range(QUARTERS):
        sl = slice(q * LANES, (q + 1) * LANES)
        dlat_ref[:part, sl] = obuf[q, 0]
        dlat_ref[part:, sl] = obuf[q, 1, part - rest : tok - rest, :]
        drope_ref[q * 16 : (q + 1) * 16, :] = obuf[q, 1, tok - rest :, :]

    for i in range(tiles):
        out_copy(i).wait()
    z2_copy().wait_send()
    z4_copy().wait_send()
    for n in range(2):
        core_copy(0, n).wait_send()
    b_copy(3, 2).wait_send()
    b_copy(1, 2).wait_send()
    b_copy(0, 1).wait_send()
    b_unread().wait_send()
    for k in (1, 2, 3):
        y_copy(k).wait_send()
        f_copy(0, k).wait_send()
        for pair in range(3):
            a1_copy(pair, k).wait_send()
    for n in range(4):
        f_copy(1, n).wait_send()
    a2_copy(1).wait_send()
    a2_copy(2).wait_send()
    a3_copy().wait_send()


def settle(*refs):
    half = (len(refs) - 2) // 3
    sems = refs[-2:]
    copies = []
    for n in range(half):
        src, dst, room = refs[n], refs[half + n], refs[2 * half + n]
        pieces = 8 if n == 0 else 1
        step = src.shape[0] // pieces
        for p in range(pieces):
            at = pl.ds(p * step, step)
            k = len(copies)
            copies.append(
                (
                    pltpu.make_async_copy(src.at[at], room.at[at], sems[0].at[k]),
                    pltpu.make_async_copy(room.at[at], dst.at[at], sems[1].at[k]),
                )
            )
    for first, _ in copies:
        first.start()
    for first, second in copies:
        first.wait()
        second.start()
    for _, second in copies:
        second.wait()


def local(query_latent, query_rope, latent, rope_key, out_grad, doc_lengths, n_ctx):
    tok, heads, width = query_latent.shape
    rope = rope_key.shape[0]
    rows = tok * heads
    keys = SLOTS * tok
    krows = tok + rope * tok // width
    half = (krows // 2 + 15) // 16 * 16
    dma = pltpu.SemaphoreType.DMA
    vmem = pltpu.VMEM
    in_vmem = pl.BlockSpec(memory_space=pltpu.VMEM)
    in_any = pl.BlockSpec(memory_space=pl.ANY)
    shapes = (
        jax.ShapeDtypeStruct((rows, width), bf16),
        jax.ShapeDtypeStruct((tok, heads * rope), bf16),
        jax.ShapeDtypeStruct((tok, width), bf16),
        jax.ShapeDtypeStruct((rope, tok), bf16),
    )
    outs = pl.pallas_call(
        functools.partial(kernel, n_ctx, heads),
        out_shape=shapes,
        in_specs=[pl.BlockSpec(memory_space=pltpu.SMEM), in_any, in_any, in_vmem, in_vmem, in_vmem],
        out_specs=(in_any, in_vmem, in_vmem, in_vmem),
        scratch_shapes=[
            vmem((rows, width), bf16),
            vmem((rows, width), bf16),
            vmem((width + LANES, rows), bf16),
            vmem((width, rows), bf16),
            vmem((rows, LANES), f32),
            vmem((rows, LANES), bf16),
            vmem((1, rows), jnp.int32),
            vmem((8, rows), f32),
            vmem((8, rows), f32),
            vmem((keys, rows), f32),
            vmem((keys, rows), f32),
            vmem((keys, rows), bf16),
            vmem((keys, rows), bf16),
            vmem((rows, width), bf16),
            vmem((SLOTS, QUARTERS, krows, LANES), bf16),
            vmem((keys, width + LANES), bf16),
            vmem((width + rope, keys), bf16),
            vmem((BLOCKS, QUARTERS, krows, LANES), bf16),
            vmem((BLOCKS, QUARTERS, half, LANES), bf16),
            vmem((QUARTERS, BLOCKS, half, LANES), bf16),
            vmem((3, BLOCKS, half, LANES), bf16),
            vmem((2, 2, half, LANES), bf16),
            vmem((2, 2, half, LANES), bf16),
            vmem((2, half, LANES), bf16),
            vmem((2, half, LANES), bf16),
            vmem((2, half, LANES), bf16),
            vmem((QUARTERS, 2, half, LANES), bf16),
            dma((2,)),
            dma((rows // TILE,)),
            dma((2,)),
            dma((2,)),
            dma((3,)),
            dma((3,)),
            dma((2,)),
            dma((2,)),
            dma((4,)),
            dma((4,)),
            dma((3, 3)),
            dma((3, 3)),
            dma((2,)),
            dma((2,)),
            dma,
            dma,
            dma((2, 4)),
            dma((2, 4)),
        ],
        compiler_params=pltpu.CompilerParams(
            collective_id=0, has_side_effects=True, vmem_limit_bytes=56 * 1024 * 1024
        ),
    )(
        doc_lengths,
        query_latent.reshape(rows, width),
        out_grad.reshape(rows, width),
        query_rope,
        latent,
        rope_key,
    )
    dq, dqr, dlat, drope = pl.pallas_call(
        settle,
        out_shape=shapes,
        in_specs=[in_any] * 4,
        out_specs=(in_any,) * 4,
        scratch_shapes=[vmem(x.shape, x.dtype) for x in shapes] + [dma((11,)), dma((11,))],
    )(*outs)
    return dq.reshape(tok, heads, width), dqr, dlat, drope


def solution(mesh):
    in_specs = (
        P("ctx", "head", None),
        P("ctx", "head"),
        P("ctx", None),
        P(None, "ctx"),
        P("ctx", "head", None),
        P(),
    )
    out_specs = (P("ctx", "head", None), P("ctx", "head"), P("ctx", None), P(None, "ctx"))
    return jax.shard_map(
        functools.partial(local, n_ctx=mesh.shape["ctx"]),
        mesh=mesh,
        in_specs=in_specs,
        out_specs=out_specs,
        check_vma=False,
    )
```

```python
import functools
import math

import jax
import jax.numpy as jnp
from jax import lax
from jax.experimental import pallas as pl
from jax.experimental.pallas import tpu as pltpu
from jax.sharding import PartitionSpec as P

MESH = pl.DeviceIdType.MESH
SPAN = 4
SLOTS = SPAN + 1
BLOCKS = SPAN + 2
QUARTERS = 4
LANES = 128
TILE = 512
softmax_scale = 192.0 ** (-0.5)
exp2_scale = softmax_scale * math.log2(math.e)
f32 = jnp.float32
bf16 = jnp.bfloat16


def kernel(
    n_ctx,
    heads,
    len_ref,
    q_hbm,
    do_hbm,
    qr_hbm,
    lat_hbm,
    rope_hbm,
    dq_hbm,
    dqr_hbm,
    dlat_hbm,
    drope_hbm,
    qr_ref,
    lat_ref,
    rope_ref,
    dqr_ref,
    dlat_ref,
    drope_ref,
    q_v,
    do_v,
    q_t,
    do_t,
    qr_f,
    qr_v,
    low_v,
    top_v,
    norm_v,
    s_v,
    dp_v,
    p_t,
    ds_t,
    dq_v,
    kbuf,
    kcat,
    k_t,
    gbuf,
    rc,
    s1,
    ry,
    sz,
    rz,
    sx,
    rx,
    fo,
    obuf,
    in_sem,
    out_sem,
    zs,
    zr,
    ys,
    yr,
    cs,
    cr,
    bs,
    br,
    a1s,
    a1r,
    a2s,
    a2r,
    a3s,
    a3r,
    fs,
    fr,
):
    rows, width = q_v.shape
    tok = lat_ref.shape[0]
    rope = rope_ref.shape[0]
    tiles = rows // TILE
    krows = kbuf.shape[2]
    part = rz.shape[3]
    rest = krows - part

    ctx = lax.axis_index("ctx")
    head = lax.axis_index("head")
    core = ctx % 2
    y = head // 2
    xh = head % 2
    sib = ctx + 1 - 2 * core

    def other_y(k):
        return (y + k) % 4

    def along(by, cross=0):
        return ((ctx + by + n_ctx) % n_ctx, y * 2 + (1 - xh if cross else xh))

    def at_y(k, c=None):
        return (ctx if c is None else c, other_y(k) * 2 + xh)

    px = (ctx, y * 2 + 1 - xh)

    def remote(src, dst, send, recv, to):
        return pltpu.make_async_remote_copy(
            src_ref=src, dst_ref=dst, send_sem=send, recv_sem=recv, device_id=to, device_id_type=MESH
        )

    in_q = pltpu.make_async_copy(q_hbm, q_v, in_sem.at[0])
    in_do = pltpu.make_async_copy(do_hbm, do_v, in_sem.at[1])
    in_lat = pltpu.make_async_copy(lat_hbm, lat_ref, in_sem.at[2])
    in_rope = pltpu.make_async_copy(rope_hbm, rope_ref, in_sem.at[3])
    in_qr = pltpu.make_async_copy(qr_hbm, qr_ref, in_sem.at[4])
    in_lat.start()
    in_rope.start()

    barrier = pltpu.get_barrier_semaphore()
    peers = [along(by, cross) for by in (-4, -2, 2, 4) for cross in (0, 1)] + [px, (sib, head)]
    for k in (1, 2, 3):
        peers += [at_y(k), at_y(k, sib)]
    for peer in peers:
        pl.semaphore_signal(barrier, inc=1, device_id=peer, device_id_type=MESH)
    in_q.start()
    in_qr.start()
    in_do.start()
    unread = (BLOCKS - 1) * core
    gbuf[unread] = jnp.zeros(gbuf.shape[1:], bf16)
    in_lat.wait()
    in_rope.wait()
    for q in range(QUARTERS):
        kbuf[0, q, :tok, :] = lat_ref[:, q * LANES : (q + 1) * LANES]
        kbuf[0, q, tok:, :] = rope_ref[q * 16 : (q + 1) * 16, :]
    pl.semaphore_wait(barrier, len(peers))

    def z4_copy():
        return remote(kbuf.at[0, y], kbuf.at[4, y], zs.at[1], zr.at[1], along(4))

    def z2_copy():
        return remote(kbuf.at[0], kbuf.at[2], zs.at[0], zr.at[0], along(2))

    def y_copy(k):
        return remote(kbuf.at[4, y], kbuf.at[4, y], ys.at[k - 1], yr.at[k - 1], at_y(k))

    def core_copy(src, n):
        return remote(kbuf.at[src], kbuf.at[1 + 2 * n], cs.at[n], cr.at[n], (sib, head))

    mine = pl.ds(pl.multiple_of(rest * core, 16), part)
    theirs = pl.ds(pl.multiple_of(rest * (1 - core), 16), part)

    def b_copy(first, count):
        b = pl.ds(first + 1 - core, count)
        n = (first + 1) // 2
        return remote(gbuf.at[b, :, theirs], rc.at[b], bs.at[n], br.at[n], (sib, head))

    def b_unread():
        return remote(gbuf.at[unread, :, theirs], rc.at[unread], bs.at[3], br.at[3], (sib, head))

    z4_copy().start()
    z2_copy().start()

    @pl.when(core == 0)
    def _():
        core_copy(0, 0).start()

    b_unread().start()

    def after_z4():
        z4_copy().wait_recv()
        for k in (2, 1, 3):
            y_copy(k).start()

    def after_z2():
        z2_copy().wait_recv()

        @pl.when(core == 0)
        def _():
            core_copy(2, 1).start()

        @pl.when(core == 1)
        def _():
            core_copy(2, 0).start()

    def after_y():
        for k in (1, 2, 3):
            y_copy(k).wait_recv()

        @pl.when(core == 1)
        def _():
            core_copy(4, 1).start()

    def unpack(slot):
        at = slot * tok
        wide = jnp.concatenate([kbuf[slot, q, :tok, :] for q in range(QUARTERS)], axis=1)
        turned = jnp.concatenate([kbuf[slot, q, tok:, :] for q in range(QUARTERS)], axis=0)
        kcat[at : at + tok, :width] = wide
        padded = jnp.concatenate([turned, jnp.zeros((LANES - rope, tok), bf16)], axis=0)
        kcat[at : at + tok, width:] = padded.T
        k_t[:width, at : at + tok] = wide.T
        k_t[width:, at : at + tok] = turned

    def lanes(i):
        return pl.ds(pl.multiple_of(i * TILE, TILE), TILE)

    def token_of(i):
        return (lax.broadcasted_iota(jnp.int32, (1, TILE), 1) + i * TILE) // heads

    def turn_q(i, c):
        q_t[:width, lanes(i)] = q_v[lanes(i), :].T
        return c

    def turn_do(i, c):
        do_t[:, lanes(i)] = do_v[lanes(i), :].T
        return c

    def turn_rope(i, c):
        block = qr_f[lanes(i), :].astype(bf16)
        qr_v[lanes(i), :] = block
        q_t[width:, lanes(i)] = block.T
        return c

    ends = []
    total = jnp.int32(0)
    for k in range(len_ref.shape[0]):
        total = total + len_ref[k]
        ends.append(total - ctx * tok)

    def first_key(i, c):
        token = token_of(i)
        low = jnp.full((1, TILE), -ctx * tok, jnp.int32)
        for end in ends:
            low = jnp.maximum(low, jnp.where(end <= token, end, low))
        low_v[:, lanes(i)] = low
        return c

    def chunk(first, count, i):
        sl = lanes(i)
        at = pl.ds(first * tok, count * tok)
        keys = kcat[at, :]
        s = jnp.dot(keys, q_t[:, sl], preferred_element_type=f32)
        dp_v[at, sl] = jnp.dot(keys[:, :width], do_t[:, sl], preferred_element_type=f32)
        low = low_v[:, sl]
        key = lax.broadcasted_iota(jnp.int32, (tok, TILE), 0)
        masked = []
        for k in range(count):
            d = first + k
            ok = key >= low + d * tok
            if d == 0:
                ok = ok & (key <= token_of(i))
            masked.append(jnp.where(ok, s[k * tok : (k + 1) * tok], -jnp.inf))
        top = jnp.full((1, TILE), -1e30, f32)
        for m in masked:
            top = jnp.maximum(top, jnp.max(m, axis=0, keepdims=True))
        norm = jnp.zeros((1, TILE), f32)
        for k in range(count):
            e = jnp.exp2((masked[k] - top) * exp2_scale)
            s_v[pl.ds((first + k) * tok, tok), sl] = e
            norm = norm + jnp.sum(e, axis=0, keepdims=True)
        top_v[first : first + 1, sl] = top
        norm_v[first : first + 1, sl] = norm

    def finish(i):
        sl = lanes(i)
        tops = [top_v[d : d + 1, sl] for d in range(SLOTS)]
        top = functools.reduce(jnp.maximum, tops)
        shares = [jnp.exp2((t - top) * exp2_scale) for t in tops]
        norm = sum(shares[d] * norm_v[d : d + 1, sl] for d in range(SLOTS))
        inverse = 1.0 / norm
        weights = [share * inverse for share in shares]
        delta = jnp.zeros((1, TILE), f32)
        for d in range(SLOTS):
            at = pl.ds(d * tok, tok)
            pb = (s_v[at, sl] * weights[d]).astype(bf16)
            p_t[at, sl] = pb
            delta = delta + jnp.sum(pb.astype(f32) * dp_v[at, sl], axis=0, keepdims=True)
        for d in range(SLOTS):
            at = pl.ds(d * tok, tok)
            scaled = weights[d] * softmax_scale
            ds_t[at, sl] = (s_v[at, sl] * scaled * (dp_v[at, sl] - delta)).astype(bf16)

    def scores(first, count):
        def body(i, c):
            chunk(first, count, i)
            return c

        lax.fori_loop(0, tiles, body, 0, unroll=4)

    def last_scores(first, count):
        def body(i, c):
            chunk(first, count, i)
            finish(i)
            return c

        lax.fori_loop(0, tiles, body, 0, unroll=4)

    in_q.wait()
    lax.fori_loop(0, tiles, turn_q, 0, unroll=4)
    qr_f[...] = jnp.zeros_like(qr_f)
    in_qr.wait()
    for h in range(heads):
        qr_f[pl.ds(h, tok, stride=heads), :rope] = qr_ref[:, h * rope : (h + 1) * rope].astype(f32)
    lax.fori_loop(0, tiles, turn_rope, 0, unroll=4)
    lax.fori_loop(0, tiles, first_key, 0)
    unpack(0)
    in_do.wait()
    lax.fori_loop(0, tiles, turn_do, 0, unroll=4)
    after_z4()
    scores(0, 1)
    after_z2()
    unpack(2)
    scores(2, 1)
    core_copy(0, 0).wait_recv()
    unpack(1)
    scores(1, 1)
    after_y()
    unpack(4)
    scores(4, 1)
    core_copy(0, 1).wait_recv()
    unpack(3)
    last_scores(3, 1)

    def key_dots(first, count):
        at = pl.ds(first * tok, count * tok)
        g = jnp.dot(p_t[at, :], do_v[...], preferred_element_type=f32)
        g = g + jnp.dot(ds_t[at, :], q_v[...], preferred_element_type=f32)
        gr = jnp.dot(ds_t[at, :], qr_v[...], preferred_element_type=f32)
        for k in range(count):
            b = first + k + 1 - core
            piece = slice(k * tok, (k + 1) * tok)
            turned = gr[piece, :].T
            for q in range(QUARTERS):
                gbuf[b, q, :tok, :] = g[piece, q * LANES : (q + 1) * LANES].astype(bf16)
                gbuf[b, q, tok:, :] = turned[q * 16 : (q + 1) * 16, :].astype(bf16)

    def key_terms(first, count):
        key_dots(first, count)
        b_copy(first, count).start()

    def a1_copy(pair, k):
        two = pl.ds(2 * pair, 2)
        return remote(
            s1.at[other_y(k), two],
            ry.at[k - 1, two],
            a1s.at[pair, k - 1],
            a1r.at[pair, k - 1],
            at_y(k),
        )

    def a2_copy(pair, cross):
        n = pair - 1
        return remote(
            sz.at[n],
            rz.at[n, cross],
            a2s.at[n, cross],
            a2r.at[n, cross],
            along(-2 * pair, cross),
        )

    def a3_copy():
        return remote(sx, rx, a3s, a3r, px)

    def red1(pair):
        if pair == 0:
            b_copy(0, 1).wait_recv()
        elif pair == 1:
            b_copy(1, 2).wait_recv()
        else:
            b_copy(3, 2).wait_recv()
            b_unread().wait_recv()
        for b in (2 * pair, 2 * pair + 1):
            for q in range(QUARTERS):
                s1[q, b] = (gbuf[b, q, mine].astype(f32) + rc[b, q].astype(f32)).astype(bf16)
        for k in (2, 1, 3):
            a1_copy(pair, k).start()

    def red2(pair):
        two = pl.ds(2 * pair, 2)
        summed = s1[y, two].astype(f32)
        for k in (1, 2, 3):
            a1_copy(pair, k).wait_recv()
            summed = summed + ry[k - 1, two].astype(f32)
        if pair:
            sz[pair - 1] = summed.astype(bf16)
            a2_copy(pair, 1).start()
            a2_copy(pair, 0).start()
        else:
            sx[...] = summed.astype(bf16)
            a3_copy().start()

    def f_copy(cross, k):
        block = core if cross else 1 - core
        return remote(
            fo.at[block],
            obuf.at[y, core],
            fs.at[cross, k],
            fr.at[cross, k],
            at_y(k, sib) if cross else at_y(k),
        )

    out_dqr = pltpu.make_async_copy(dqr_ref, dqr_hbm, out_sem.at[tiles])
    out_dlat = pltpu.make_async_copy(dlat_ref, dlat_hbm, out_sem.at[tiles + 1])
    out_drope = pltpu.make_async_copy(drope_ref, drope_hbm, out_sem.at[tiles + 2])

    def out_copy(i):
        return pltpu.make_async_copy(dq_v.at[lanes(i)], dq_hbm.at[lanes(i)], out_sem.at[i])

    def query_terms(i, c):
        sl = lanes(i)
        turned = jnp.dot(k_t[...], ds_t[:, sl], preferred_element_type=f32)
        dq_v[sl, :] = turned[:width, :].astype(bf16).T
        qr_f[sl, :rope] = turned[width:, :].T
        out_copy(i).start()
        return c

    def query_run(first, last):
        lax.fori_loop(first, last, query_terms, 0)

    key_terms(3, 2)
    key_terms(1, 2)
    red1(2)
    key_terms(0, 1)
    red1(1)
    query_run(0, 1)
    red1(0)
    query_run(1, tiles // 2)
    red2(2)
    red2(1)
    red2(0)
    query_run(tiles // 2, tiles)

    a3_copy().wait_recv()
    summed = sx[...].astype(f32) + rx[...].astype(f32)
    for pair in (2, 1):
        for cross in (0, 1):
            a2_copy(pair, cross).wait_recv()
        summed = summed + (rz[pair - 1, 0].astype(f32) + rz[pair - 1, 1].astype(f32))
    fo[...] = summed.astype(bf16)
    for k in (2, 1, 3):
        f_copy(0, k).start()
        f_copy(1, k).start()
    f_copy(1, 0).start()
    obuf[y, core] = fo[1 - core]
    for h in range(heads):
        dqr_ref[:, h * rope : (h + 1) * rope] = qr_f[pl.ds(h, tok, stride=heads), :rope].astype(bf16)
    out_dqr.start()
    for k in range(4):
        f_copy(1, k).wait_recv()
        if k:
            f_copy(0, k).wait_recv()
    for q in range(QUARTERS):
        sl = slice(q * LANES, (q + 1) * LANES)
        dlat_ref[:part, sl] = obuf[q, 0]
        dlat_ref[part:, sl] = obuf[q, 1, part - rest : tok - rest, :]
        drope_ref[q * 16 : (q + 1) * 16, :] = obuf[q, 1, tok - rest :, :]

    out_dlat.start()
    out_drope.start()
    for i in range(tiles):
        out_copy(i).wait()
    z2_copy().wait_send()
    z4_copy().wait_send()
    for n in range(2):
        core_copy(0, n).wait_send()
    b_copy(3, 2).wait_send()
    b_copy(1, 2).wait_send()
    b_copy(0, 1).wait_send()
    b_unread().wait_send()
    for k in (1, 2, 3):
        y_copy(k).wait_send()
        f_copy(0, k).wait_send()
        for pair in range(3):
            a1_copy(pair, k).wait_send()
    for n in range(4):
        f_copy(1, n).wait_send()
    for cross in (0, 1):
        a2_copy(1, cross).wait_send()
        a2_copy(2, cross).wait_send()
    a3_copy().wait_send()
    out_dqr.wait()
    out_dlat.wait()
    out_drope.wait()


def settle(*refs):
    half = (len(refs) - 2) // 3
    sems = refs[-2:]
    copies = []
    for n in range(half):
        src, dst, room = refs[n], refs[half + n], refs[2 * half + n]
        pieces = 8 if n == 0 else 1
        step = src.shape[0] // pieces
        for p in range(pieces):
            at = pl.ds(p * step, step)
            k = len(copies)
            copies.append(
                (
                    pltpu.make_async_copy(src.at[at], room.at[at], sems[0].at[k]),
                    pltpu.make_async_copy(room.at[at], dst.at[at], sems[1].at[k]),
                )
            )
    for first, _ in copies:
        first.start()
    for first, second in copies:
        first.wait()
        second.start()
    for _, second in copies:
        second.wait()


def local(query_latent, query_rope, latent, rope_key, out_grad, doc_lengths, n_ctx):
    tok, heads, width = query_latent.shape
    rope = rope_key.shape[0]
    rows = tok * heads
    keys = SLOTS * tok
    krows = tok + rope * tok // width
    half = (krows // 2 + 15) // 16 * 16
    dma = pltpu.SemaphoreType.DMA
    vmem = pltpu.VMEM
    in_any = pl.BlockSpec(memory_space=pl.ANY)
    shapes = (
        jax.ShapeDtypeStruct((rows, width), bf16),
        jax.ShapeDtypeStruct((tok, heads * rope), bf16),
        jax.ShapeDtypeStruct((tok, width), bf16),
        jax.ShapeDtypeStruct((rope, tok), bf16),
    )
    outs = pl.pallas_call(
        functools.partial(kernel, n_ctx, heads),
        out_shape=shapes,
        in_specs=[pl.BlockSpec(memory_space=pltpu.SMEM), in_any, in_any, in_any, in_any, in_any],
        out_specs=(in_any,) * 4,
        scratch_shapes=[
            vmem((tok, heads * rope), bf16),
            vmem((tok, width), bf16),
            vmem((rope, tok), bf16),
            vmem((tok, heads * rope), bf16),
            vmem((tok, width), bf16),
            vmem((rope, tok), bf16),
            vmem((rows, width), bf16),
            vmem((rows, width), bf16),
            vmem((width + LANES, rows), bf16),
            vmem((width, rows), bf16),
            vmem((rows, LANES), f32),
            vmem((rows, LANES), bf16),
            vmem((1, rows), jnp.int32),
            vmem((8, rows), f32),
            vmem((8, rows), f32),
            vmem((keys, rows), f32),
            vmem((keys, rows), f32),
            vmem((keys, rows), bf16),
            vmem((keys, rows), bf16),
            vmem((rows, width), bf16),
            vmem((SLOTS, QUARTERS, krows, LANES), bf16),
            vmem((keys, width + LANES), bf16),
            vmem((width + rope, keys), bf16),
            vmem((BLOCKS, QUARTERS, krows, LANES), bf16),
            vmem((BLOCKS, QUARTERS, half, LANES), bf16),
            vmem((QUARTERS, BLOCKS, half, LANES), bf16),
            vmem((3, BLOCKS, half, LANES), bf16),
            vmem((2, 2, half, LANES), bf16),
            vmem((2, 2, 2, half, LANES), bf16),
            vmem((2, half, LANES), bf16),
            vmem((2, half, LANES), bf16),
            vmem((2, half, LANES), bf16),
            vmem((QUARTERS, 2, half, LANES), bf16),
            dma((5,)),
            dma((rows // TILE + 3,)),
            dma((2,)),
            dma((2,)),
            dma((3,)),
            dma((3,)),
            dma((2,)),
            dma((2,)),
            dma((4,)),
            dma((4,)),
            dma((3, 3)),
            dma((3, 3)),
            dma((2, 2)),
            dma((2, 2)),
            dma,
            dma,
            dma((2, 4)),
            dma((2, 4)),
        ],
        compiler_params=pltpu.CompilerParams(
            collective_id=0, has_side_effects=True, vmem_limit_bytes=56 * 1024 * 1024
        ),
    )(
        doc_lengths,
        query_latent.reshape(rows, width),
        out_grad.reshape(rows, width),
        query_rope,
        latent,
        rope_key,
    )
    dq, dqr, dlat, drope = pl.pallas_call(
        settle,
        out_shape=shapes,
        in_specs=[in_any] * 4,
        out_specs=(in_any,) * 4,
        scratch_shapes=[vmem(x.shape, x.dtype) for x in shapes] + [dma((11,)), dma((11,))],
    )(*outs)
    return dq.reshape(tok, heads, width), dqr, dlat, drope


def solution(mesh):
    in_specs = (
        P("ctx", "head", None),
        P("ctx", "head"),
        P("ctx", None),
        P(None, "ctx"),
        P("ctx", "head", None),
        P(),
    )
    out_specs = (P("ctx", "head", None), P("ctx", "head"), P("ctx", None), P(None, "ctx"))
    return jax.shard_map(
        functools.partial(local, n_ctx=mesh.shape["ctx"]),
        mesh=mesh,
        in_specs=in_specs,
        out_specs=out_specs,
        check_vma=False,
    )
```

```python
import functools
import math

import jax
import jax.numpy as jnp
from jax import lax
from jax.experimental import pallas as pl
from jax.experimental.pallas import tpu as pltpu
from jax.sharding import PartitionSpec as P

MESH = pl.DeviceIdType.MESH
SPAN = 4
SLOTS = SPAN + 1
BLOCKS = SPAN + 2
QUARTERS = 4
LANES = 128
TILE = 512
softmax_scale = 192.0 ** (-0.5)
exp2_scale = softmax_scale * math.log2(math.e)
f32 = jnp.float32
bf16 = jnp.bfloat16


def kernel(
    n_ctx,
    heads,
    len_ref,
    q_hbm,
    do_hbm,
    qr_hbm,
    lat_hbm,
    rope_hbm,
    dq_v,
    dqr_ref,
    dlat_ref,
    drope_ref,
    qr_ref,
    lat_ref,
    rope_ref,
    q_v,
    do_v,
    q_t,
    do_t,
    qr_f,
    qr_v,
    low_v,
    top_v,
    norm_v,
    s_v,
    dp_v,
    p_t,
    ds_t,
    kbuf,
    kcat,
    k_t,
    gbuf,
    rc,
    s1,
    ry,
    sz,
    rz,
    sx,
    rx,
    fo,
    obuf,
    in_sem,
    zs,
    zr,
    ys,
    yr,
    cs,
    cr,
    bs,
    br,
    a1s,
    a1r,
    a2s,
    a2r,
    a3s,
    a3r,
    fs,
    fr,
):
    rows, width = q_v.shape
    tok = lat_ref.shape[0]
    rope = rope_ref.shape[0]
    tiles = rows // TILE
    krows = kbuf.shape[2]
    part = rz.shape[3]
    rest = krows - part

    ctx = lax.axis_index("ctx")
    head = lax.axis_index("head")
    core = ctx % 2
    y = head // 2
    xh = head % 2
    sib = ctx + 1 - 2 * core

    def other_y(k):
        return (y + k) % 4

    def along(by, cross=0):
        return ((ctx + by + n_ctx) % n_ctx, y * 2 + (1 - xh if cross else xh))

    def at_y(k, c=None):
        return (ctx if c is None else c, other_y(k) * 2 + xh)

    px = (ctx, y * 2 + 1 - xh)

    def remote(src, dst, send, recv, to):
        return pltpu.make_async_remote_copy(
            src_ref=src, dst_ref=dst, send_sem=send, recv_sem=recv, device_id=to, device_id_type=MESH
        )

    in_q = pltpu.make_async_copy(q_hbm, q_v, in_sem.at[0])
    in_do = pltpu.make_async_copy(do_hbm, do_v, in_sem.at[1])
    in_lat = pltpu.make_async_copy(lat_hbm, lat_ref, in_sem.at[2])
    in_rope = pltpu.make_async_copy(rope_hbm, rope_ref, in_sem.at[3])
    in_qr = pltpu.make_async_copy(qr_hbm, qr_ref, in_sem.at[4])
    in_lat.start()
    in_rope.start()

    barrier = pltpu.get_barrier_semaphore()
    peers = [along(by, cross) for by in (-4, -2, 2, 4) for cross in (0, 1)] + [px, (sib, head)]
    for k in (1, 2, 3):
        peers += [at_y(k), at_y(k, sib)]
    for peer in peers:
        pl.semaphore_signal(barrier, inc=1, device_id=peer, device_id_type=MESH)
    in_q.start()
    in_qr.start()
    in_do.start()
    unread = (BLOCKS - 1) * core
    gbuf[unread] = jnp.zeros(gbuf.shape[1:], bf16)
    in_lat.wait()
    in_rope.wait()
    for q in range(QUARTERS):
        kbuf[0, q, :tok, :] = lat_ref[:, q * LANES : (q + 1) * LANES]
        kbuf[0, q, tok:, :] = rope_ref[q * 16 : (q + 1) * 16, :]
    pl.semaphore_wait(barrier, len(peers))

    def z4_copy():
        return remote(kbuf.at[0, y], kbuf.at[4, y], zs.at[1], zr.at[1], along(4))

    def z2_copy():
        return remote(kbuf.at[0], kbuf.at[2], zs.at[0], zr.at[0], along(2))

    def y_copy(k):
        return remote(kbuf.at[4, y], kbuf.at[4, y], ys.at[k - 1], yr.at[k - 1], at_y(k))

    def core_copy(src, n):
        return remote(kbuf.at[src], kbuf.at[1 + 2 * n], cs.at[n], cr.at[n], (sib, head))

    mine = pl.ds(pl.multiple_of(rest * core, 16), part)
    theirs = pl.ds(pl.multiple_of(rest * (1 - core), 16), part)

    def b_copy(first, count):
        b = pl.ds(first + 1 - core, count)
        n = (first + 1) // 2
        return remote(gbuf.at[b, :, theirs], rc.at[b], bs.at[n], br.at[n], (sib, head))

    def b_unread():
        return remote(gbuf.at[unread, :, theirs], rc.at[unread], bs.at[3], br.at[3], (sib, head))

    z4_copy().start()
    z2_copy().start()

    @pl.when(core == 0)
    def _():
        core_copy(0, 0).start()

    b_unread().start()

    def after_z4():
        z4_copy().wait_recv()
        for k in (2, 1, 3):
            y_copy(k).start()

    def after_z2():
        z2_copy().wait_recv()

        @pl.when(core == 0)
        def _():
            core_copy(2, 1).start()

        @pl.when(core == 1)
        def _():
            core_copy(2, 0).start()

    def after_y():
        for k in (1, 2, 3):
            y_copy(k).wait_recv()

        @pl.when(core == 1)
        def _():
            core_copy(4, 1).start()

    def unpack(slot):
        at = slot * tok
        wide = jnp.concatenate([kbuf[slot, q, :tok, :] for q in range(QUARTERS)], axis=1)
        turned = jnp.concatenate([kbuf[slot, q, tok:, :] for q in range(QUARTERS)], axis=0)
        kcat[at : at + tok, :width] = wide
        padded = jnp.concatenate([turned, jnp.zeros((LANES - rope, tok), bf16)], axis=0)
        kcat[at : at + tok, width:] = padded.T
        k_t[:width, at : at + tok] = wide.T
        k_t[width:, at : at + tok] = turned

    def lanes(i):
        return pl.ds(pl.multiple_of(i * TILE, TILE), TILE)

    def token_of(i):
        return (lax.broadcasted_iota(jnp.int32, (1, TILE), 1) + i * TILE) // heads

    def turn_q(i, c):
        q_t[:width, lanes(i)] = q_v[lanes(i), :].T
        return c

    def turn_do(i, c):
        do_t[:, lanes(i)] = do_v[lanes(i), :].T
        return c

    def turn_rope(i, c):
        block = qr_f[lanes(i), :].astype(bf16)
        qr_v[lanes(i), :] = block
        q_t[width:, lanes(i)] = block.T
        return c

    ends = []
    total = jnp.int32(0)
    for k in range(len_ref.shape[0]):
        total = total + len_ref[k]
        ends.append(total - ctx * tok)

    def first_key(i, c):
        token = token_of(i)
        low = jnp.full((1, TILE), -ctx * tok, jnp.int32)
        for end in ends:
            low = jnp.maximum(low, jnp.where(end <= token, end, low))
        low_v[:, lanes(i)] = low
        return c

    def chunk(first, count, i):
        sl = lanes(i)
        at = pl.ds(first * tok, count * tok)
        keys = kcat[at, :]
        s = jnp.dot(keys, q_t[:, sl], preferred_element_type=f32)
        dp_v[at, sl] = jnp.dot(keys[:, :width], do_t[:, sl], preferred_element_type=f32)
        low = low_v[:, sl]
        key = lax.broadcasted_iota(jnp.int32, (tok, TILE), 0)
        masked = []
        for k in range(count):
            d = first + k
            ok = key >= low + d * tok
            if d == 0:
                ok = ok & (key <= token_of(i))
            masked.append(jnp.where(ok, s[k * tok : (k + 1) * tok], -jnp.inf))
        top = jnp.full((1, TILE), -1e30, f32)
        for m in masked:
            top = jnp.maximum(top, jnp.max(m, axis=0, keepdims=True))
        norm = jnp.zeros((1, TILE), f32)
        for k in range(count):
            e = jnp.exp2((masked[k] - top) * exp2_scale)
            s_v[pl.ds((first + k) * tok, tok), sl] = e
            norm = norm + jnp.sum(e, axis=0, keepdims=True)
        top_v[first : first + 1, sl] = top
        norm_v[first : first + 1, sl] = norm

    def finish(i):
        sl = lanes(i)
        tops = [top_v[d : d + 1, sl] for d in range(SLOTS)]
        top = functools.reduce(jnp.maximum, tops)
        shares = [jnp.exp2((t - top) * exp2_scale) for t in tops]
        norm = sum(shares[d] * norm_v[d : d + 1, sl] for d in range(SLOTS))
        inverse = 1.0 / norm
        weights = [share * inverse for share in shares]
        delta = jnp.zeros((1, TILE), f32)
        for d in range(SLOTS):
            at = pl.ds(d * tok, tok)
            pb = (s_v[at, sl] * weights[d]).astype(bf16)
            p_t[at, sl] = pb
            delta = delta + jnp.sum(pb.astype(f32) * dp_v[at, sl], axis=0, keepdims=True)
        for d in range(SLOTS):
            at = pl.ds(d * tok, tok)
            scaled = weights[d] * softmax_scale
            ds_t[at, sl] = (s_v[at, sl] * scaled * (dp_v[at, sl] - delta)).astype(bf16)

    def scores(first, count):
        def body(i, c):
            chunk(first, count, i)
            return c

        lax.fori_loop(0, tiles, body, 0, unroll=4)

    def last_scores(first, count):
        def body(i, c):
            chunk(first, count, i)
            finish(i)
            return c

        lax.fori_loop(0, tiles, body, 0, unroll=4)

    in_q.wait()
    lax.fori_loop(0, tiles, turn_q, 0, unroll=4)
    qr_f[...] = jnp.zeros_like(qr_f)
    in_qr.wait()
    for h in range(heads):
        qr_f[pl.ds(h, tok, stride=heads), :rope] = qr_ref[:, h * rope : (h + 1) * rope].astype(f32)
    lax.fori_loop(0, tiles, turn_rope, 0, unroll=4)
    lax.fori_loop(0, tiles, first_key, 0)
    unpack(0)
    in_do.wait()
    lax.fori_loop(0, tiles, turn_do, 0, unroll=4)
    after_z4()
    scores(0, 1)
    after_z2()
    unpack(2)
    scores(2, 1)
    core_copy(0, 0).wait_recv()
    unpack(1)
    scores(1, 1)
    after_y()
    unpack(4)
    scores(4, 1)
    core_copy(0, 1).wait_recv()
    unpack(3)
    last_scores(3, 1)

    def key_dots(first, count):
        at = pl.ds(first * tok, count * tok)
        g = jnp.dot(p_t[at, :], do_v[...], preferred_element_type=f32)
        g = g + jnp.dot(ds_t[at, :], q_v[...], preferred_element_type=f32)
        gr = jnp.dot(ds_t[at, :], qr_v[...], preferred_element_type=f32)
        for k in range(count):
            b = first + k + 1 - core
            piece = slice(k * tok, (k + 1) * tok)
            turned = gr[piece, :].T
            for q in range(QUARTERS):
                gbuf[b, q, :tok, :] = g[piece, q * LANES : (q + 1) * LANES].astype(bf16)
                gbuf[b, q, tok:, :] = turned[q * 16 : (q + 1) * 16, :].astype(bf16)

    def key_terms(first, count):
        key_dots(first, count)
        b_copy(first, count).start()

    def a1_copy(pair, k):
        two = pl.ds(2 * pair, 2)
        return remote(
            s1.at[other_y(k), two],
            ry.at[k - 1, two],
            a1s.at[pair, k - 1],
            a1r.at[pair, k - 1],
            at_y(k),
        )

    def a2_copy(pair, cross):
        n = pair - 1
        return remote(
            sz.at[n],
            rz.at[n, cross],
            a2s.at[n, cross],
            a2r.at[n, cross],
            along(-2 * pair, cross),
        )

    def a3_copy():
        return remote(sx, rx, a3s, a3r, px)

    def red1(pair):
        if pair == 0:
            b_copy(0, 1).wait_recv()
        elif pair == 1:
            b_copy(1, 2).wait_recv()
        else:
            b_copy(3, 2).wait_recv()
            b_unread().wait_recv()
        for b in (2 * pair, 2 * pair + 1):
            for q in range(QUARTERS):
                s1[q, b] = (gbuf[b, q, mine].astype(f32) + rc[b, q].astype(f32)).astype(bf16)
        for k in (2, 1, 3):
            a1_copy(pair, k).start()

    def red2(pair):
        two = pl.ds(2 * pair, 2)
        summed = s1[y, two].astype(f32)
        for k in (1, 2, 3):
            a1_copy(pair, k).wait_recv()
            summed = summed + ry[k - 1, two].astype(f32)
        if pair:
            sz[pair - 1] = summed.astype(bf16)
            a2_copy(pair, 1).start()
            a2_copy(pair, 0).start()
        else:
            sx[...] = summed.astype(bf16)
            a3_copy().start()

    def f_copy(cross, k):
        block = core if cross else 1 - core
        return remote(
            fo.at[block],
            obuf.at[y, core],
            fs.at[cross, k],
            fr.at[cross, k],
            at_y(k, sib) if cross else at_y(k),
        )

    def query_terms(i, c):
        sl = lanes(i)
        turned = jnp.dot(k_t[...], ds_t[:, sl], preferred_element_type=f32)
        dq_v[sl, :] = turned[:width, :].astype(bf16).T
        qr_f[sl, :rope] = turned[width:, :].T
        return c

    def query_run(first, last):
        lax.fori_loop(first, last, query_terms, 0)

    key_terms(3, 2)
    key_terms(1, 2)
    red1(2)
    key_terms(0, 1)
    red1(1)
    query_run(0, 1)
    red1(0)
    query_run(1, tiles // 2)
    red2(2)
    red2(1)
    red2(0)
    query_run(tiles // 2, tiles)

    a3_copy().wait_recv()
    summed = sx[...].astype(f32) + rx[...].astype(f32)
    for pair in (2, 1):
        for cross in (0, 1):
            a2_copy(pair, cross).wait_recv()
        summed = summed + (rz[pair - 1, 0].astype(f32) + rz[pair - 1, 1].astype(f32))
    fo[...] = summed.astype(bf16)
    for k in (2, 1, 3):
        f_copy(0, k).start()
        f_copy(1, k).start()
    f_copy(1, 0).start()
    obuf[y, core] = fo[1 - core]
    for h in range(heads):
        dqr_ref[:, h * rope : (h + 1) * rope] = qr_f[pl.ds(h, tok, stride=heads), :rope].astype(bf16)
    for k in range(4):
        f_copy(1, k).wait_recv()
        if k:
            f_copy(0, k).wait_recv()
    for q in range(QUARTERS):
        sl = slice(q * LANES, (q + 1) * LANES)
        dlat_ref[:part, sl] = obuf[q, 0]
        dlat_ref[part:, sl] = obuf[q, 1, part - rest : tok - rest, :]
        drope_ref[q * 16 : (q + 1) * 16, :] = obuf[q, 1, tok - rest :, :]

    z2_copy().wait_send()
    z4_copy().wait_send()
    for n in range(2):
        core_copy(0, n).wait_send()
    b_copy(3, 2).wait_send()
    b_copy(1, 2).wait_send()
    b_copy(0, 1).wait_send()
    b_unread().wait_send()
    for k in (1, 2, 3):
        y_copy(k).wait_send()
        f_copy(0, k).wait_send()
        for pair in range(3):
            a1_copy(pair, k).wait_send()
    for n in range(4):
        f_copy(1, n).wait_send()
    for cross in (0, 1):
        a2_copy(1, cross).wait_send()
        a2_copy(2, cross).wait_send()
    a3_copy().wait_send()


def settle(*refs):
    half = (len(refs) - 1) // 2
    sems = refs[-1]
    copies = []
    for n in range(half):
        src, dst = refs[n], refs[half + n]
        pieces = 8 if n == 0 else 1
        step = src.shape[0] // pieces
        for p in range(pieces):
            at = pl.ds(p * step, step)
            copies.append(pltpu.make_async_copy(src.at[at], dst.at[at], sems.at[len(copies)]))
    for copy in copies:
        copy.start()
    for copy in copies:
        copy.wait()


def local(query_latent, query_rope, latent, rope_key, out_grad, doc_lengths, n_ctx):
    tok, heads, width = query_latent.shape
    rope = rope_key.shape[0]
    rows = tok * heads
    keys = SLOTS * tok
    krows = tok + rope * tok // width
    half = (krows // 2 + 15) // 16 * 16
    dma = pltpu.SemaphoreType.DMA
    vmem = pltpu.VMEM
    in_any = pl.BlockSpec(memory_space=pl.ANY)
    shapes = (
        jax.ShapeDtypeStruct((rows, width), bf16),
        jax.ShapeDtypeStruct((tok, heads * rope), bf16),
        jax.ShapeDtypeStruct((tok, width), bf16),
        jax.ShapeDtypeStruct((rope, tok), bf16),
    )
    outs = pl.pallas_call(
        functools.partial(kernel, n_ctx, heads),
        out_shape=tuple(vmem(x.shape, x.dtype) for x in shapes),
        in_specs=[pl.BlockSpec(memory_space=pltpu.SMEM), in_any, in_any, in_any, in_any, in_any],
        out_specs=(pl.BlockSpec(memory_space=pltpu.VMEM),) * 4,
        scratch_shapes=[
            vmem((tok, heads * rope), bf16),
            vmem((tok, width), bf16),
            vmem((rope, tok), bf16),
            vmem((rows, width), bf16),
            vmem((rows, width), bf16),
            vmem((width + LANES, rows), bf16),
            vmem((width, rows), bf16),
            vmem((rows, LANES), f32),
            vmem((rows, LANES), bf16),
            vmem((1, rows), jnp.int32),
            vmem((8, rows), f32),
            vmem((8, rows), f32),
            vmem((keys, rows), f32),
            vmem((keys, rows), f32),
            vmem((keys, rows), bf16),
            vmem((keys, rows), bf16),
            vmem((SLOTS, QUARTERS, krows, LANES), bf16),
            vmem((keys, width + LANES), bf16),
            vmem((width + rope, keys), bf16),
            vmem((BLOCKS, QUARTERS, krows, LANES), bf16),
            vmem((BLOCKS, QUARTERS, half, LANES), bf16),
            vmem((QUARTERS, BLOCKS, half, LANES), bf16),
            vmem((3, BLOCKS, half, LANES), bf16),
            vmem((2, 2, half, LANES), bf16),
            vmem((2, 2, 2, half, LANES), bf16),
            vmem((2, half, LANES), bf16),
            vmem((2, half, LANES), bf16),
            vmem((2, half, LANES), bf16),
            vmem((QUARTERS, 2, half, LANES), bf16),
            dma((5,)),
            dma((2,)),
            dma((2,)),
            dma((3,)),
            dma((3,)),
            dma((2,)),
            dma((2,)),
            dma((4,)),
            dma((4,)),
            dma((3, 3)),
            dma((3, 3)),
            dma((2, 2)),
            dma((2, 2)),
            dma,
            dma,
            dma((2, 4)),
            dma((2, 4)),
        ],
        compiler_params=pltpu.CompilerParams(
            collective_id=0, has_side_effects=True, vmem_limit_bytes=56 * 1024 * 1024
        ),
    )(
        doc_lengths,
        query_latent.reshape(rows, width),
        out_grad.reshape(rows, width),
        query_rope,
        latent,
        rope_key,
    )
    dq, dqr, dlat, drope = pl.pallas_call(
        settle,
        out_shape=shapes,
        in_specs=[in_any] * 4,
        out_specs=(in_any,) * 4,
        scratch_shapes=[dma((11,))],
        compiler_params=pltpu.CompilerParams(vmem_limit_bytes=1024 * 1024),
    )(*outs)
    return dq.reshape(tok, heads, width), dqr, dlat, drope


def solution(mesh):
    in_specs = (
        P("ctx", "head", None),
        P("ctx", "head"),
        P("ctx", None),
        P(None, "ctx"),
        P("ctx", "head", None),
        P(),
    )
    out_specs = (P("ctx", "head", None), P("ctx", "head"), P("ctx", None), P(None, "ctx"))
    return jax.shard_map(
        functools.partial(local, n_ctx=mesh.shape["ctx"]),
        mesh=mesh,
        in_specs=in_specs,
        out_specs=out_specs,
        check_vma=False,
    )
```

```python
import functools
import math

import jax
import jax.numpy as jnp
from jax import lax
from jax.experimental import pallas as pl
from jax.experimental.pallas import tpu as pltpu
from jax.sharding import PartitionSpec as P

MESH = pl.DeviceIdType.MESH
SPAN = 4
SLOTS = SPAN + 1
BLOCKS = SPAN + 2
QUARTERS = 4
LANES = 128
TILE = 512
softmax_scale = 192.0 ** (-0.5)
exp2_scale = softmax_scale * math.log2(math.e)
f32 = jnp.float32
bf16 = jnp.bfloat16


def kernel(
    n_ctx,
    heads,
    len_ref,
    q_hbm,
    do_hbm,
    qr_hbm,
    lat_hbm,
    rope_hbm,
    dq_v,
    dqr_ref,
    dlat_ref,
    drope_ref,
    qr_ref,
    lat_ref,
    rope_ref,
    q_v,
    do_v,
    q_t,
    do_t,
    qr_f,
    qr_v,
    low_v,
    top_v,
    norm_v,
    s_v,
    dp_v,
    p_t,
    ds_t,
    kbuf,
    kcat,
    k_t,
    gbuf,
    rc,
    s1,
    ry,
    sz,
    rz,
    sx,
    rx,
    fo,
    obuf,
    in_sem,
    zs,
    zr,
    ys,
    yr,
    cs,
    cr,
    bs,
    br,
    a1s,
    a1r,
    a2s,
    a2r,
    a3s,
    a3r,
    fs,
    fr,
):
    rows, width = q_v.shape
    tok = lat_ref.shape[0]
    rope = rope_ref.shape[0]
    tiles = rows // TILE
    krows = kbuf.shape[2]
    part = rz.shape[3]
    rest = krows - part

    ctx = lax.axis_index("ctx")
    head = lax.axis_index("head")
    core = ctx % 2
    y = head // 2
    xh = head % 2
    sib = ctx + 1 - 2 * core

    def other_y(k):
        return (y + k) % 4

    def along(by, cross=0):
        return ((ctx + by + n_ctx) % n_ctx, y * 2 + (1 - xh if cross else xh))

    def at_y(k, c=None):
        return (ctx if c is None else c, other_y(k) * 2 + xh)

    px = (ctx, y * 2 + 1 - xh)

    def remote(src, dst, send, recv, to):
        return pltpu.make_async_remote_copy(
            src_ref=src, dst_ref=dst, send_sem=send, recv_sem=recv, device_id=to, device_id_type=MESH
        )

    in_q = pltpu.make_async_copy(q_hbm, q_v, in_sem.at[0])
    in_do = pltpu.make_async_copy(do_hbm, do_v, in_sem.at[1])
    in_lat = pltpu.make_async_copy(lat_hbm, lat_ref, in_sem.at[2])
    in_rope = pltpu.make_async_copy(rope_hbm, rope_ref, in_sem.at[3])
    in_qr = pltpu.make_async_copy(qr_hbm, qr_ref, in_sem.at[4])
    in_lat.start()
    in_rope.start()

    barrier = pltpu.get_barrier_semaphore()
    peers = [along(by, cross) for by in (-4, -2, 2, 4) for cross in (0, 1)] + [px, (sib, head)]
    for k in (1, 2, 3):
        peers += [at_y(k), at_y(k, sib)]
    for peer in peers:
        pl.semaphore_signal(barrier, inc=1, device_id=peer, device_id_type=MESH)
    in_q.start()
    in_qr.start()
    in_do.start()
    unread = (BLOCKS - 1) * core
    gbuf[unread] = jnp.zeros(gbuf.shape[1:], bf16)
    in_lat.wait()
    in_rope.wait()
    for q in range(QUARTERS):
        kbuf[0, q, :tok, :] = lat_ref[:, q * LANES : (q + 1) * LANES]
        kbuf[0, q, tok:, :] = rope_ref[q * 16 : (q + 1) * 16, :]
    pl.semaphore_wait(barrier, len(peers))

    def z4_copy():
        return remote(kbuf.at[0, y], kbuf.at[4, y], zs.at[1], zr.at[1], along(4))

    def z2_copy():
        return remote(kbuf.at[0], kbuf.at[2], zs.at[0], zr.at[0], along(2))

    def y_copy(k):
        return remote(kbuf.at[4, y], kbuf.at[4, y], ys.at[k - 1], yr.at[k - 1], at_y(k))

    def core_copy(src, n):
        return remote(kbuf.at[src], kbuf.at[1 + 2 * n], cs.at[n], cr.at[n], (sib, head))

    mine = pl.ds(pl.multiple_of(rest * core, 16), part)
    theirs = pl.ds(pl.multiple_of(rest * (1 - core), 16), part)

    def b_copy(first, count):
        b = pl.ds(first + 1 - core, count)
        n = (first + 1) // 2
        return remote(gbuf.at[b, :, theirs], rc.at[b], bs.at[n], br.at[n], (sib, head))

    def b_unread():
        return remote(gbuf.at[unread, :, theirs], rc.at[unread], bs.at[3], br.at[3], (sib, head))

    z4_copy().start()
    z2_copy().start()

    @pl.when(core == 0)
    def _():
        core_copy(0, 0).start()

    b_unread().start()

    def after_z4():
        z4_copy().wait_recv()
        for k in (2, 1, 3):
            y_copy(k).start()

    def after_z2():
        z2_copy().wait_recv()

        @pl.when(core == 0)
        def _():
            core_copy(2, 1).start()

        @pl.when(core == 1)
        def _():
            core_copy(2, 0).start()

    def after_y():
        for k in (1, 2, 3):
            y_copy(k).wait_recv()

        @pl.when(core == 1)
        def _():
            core_copy(4, 1).start()

    def unpack(slot):
        at = slot * tok
        wide = jnp.concatenate([kbuf[slot, q, :tok, :] for q in range(QUARTERS)], axis=1)
        turned = jnp.concatenate([kbuf[slot, q, tok:, :] for q in range(QUARTERS)], axis=0)
        kcat[at : at + tok, :width] = wide
        padded = jnp.concatenate([turned, jnp.zeros((LANES - rope, tok), bf16)], axis=0)
        kcat[at : at + tok, width:] = padded.T
        k_t[:width, at : at + tok] = wide.T
        k_t[width:, at : at + tok] = turned

    def lanes(i):
        return pl.ds(pl.multiple_of(i * TILE, TILE), TILE)

    def token_of(i):
        return (lax.broadcasted_iota(jnp.int32, (1, TILE), 1) + i * TILE) // heads

    def turn_q(i, c):
        q_t[:width, lanes(i)] = q_v[lanes(i), :].T
        return c

    def turn_do(i, c):
        do_t[:, lanes(i)] = do_v[lanes(i), :].T
        return c

    def turn_rope(i, c):
        block = qr_f[lanes(i), :].astype(bf16)
        qr_v[lanes(i), :] = block
        q_t[width:, lanes(i)] = block.T
        return c

    ends = []
    total = jnp.int32(0)
    for k in range(len_ref.shape[0]):
        total = total + len_ref[k]
        ends.append(total - ctx * tok)

    def first_key(i, c):
        token = token_of(i)
        low = jnp.full((1, TILE), -ctx * tok, jnp.int32)
        for end in ends:
            low = jnp.maximum(low, jnp.where(end <= token, end, low))
        low_v[:, lanes(i)] = low
        return c

    def chunk(first, count, i):
        sl = lanes(i)
        at = pl.ds(first * tok, count * tok)
        keys = kcat[at, :]
        s = jnp.dot(keys, q_t[:, sl], preferred_element_type=f32)
        dp_v[at, sl] = jnp.dot(keys[:, :width], do_t[:, sl], preferred_element_type=f32)
        low = low_v[:, sl]
        key = lax.broadcasted_iota(jnp.int32, (tok, TILE), 0)
        masked = []
        for k in range(count):
            d = first + k
            ok = key >= low + d * tok
            if d == 0:
                ok = ok & (key <= token_of(i))
            masked.append(jnp.where(ok, s[k * tok : (k + 1) * tok], -jnp.inf))
        top = jnp.full((1, TILE), -1e30, f32)
        for m in masked:
            top = jnp.maximum(top, jnp.max(m, axis=0, keepdims=True))
        norm = jnp.zeros((1, TILE), f32)
        for k in range(count):
            e = jnp.exp2((masked[k] - top) * exp2_scale)
            s_v[pl.ds((first + k) * tok, tok), sl] = e
            norm = norm + jnp.sum(e, axis=0, keepdims=True)
        top_v[first : first + 1, sl] = top
        norm_v[first : first + 1, sl] = norm

    def finish(i):
        sl = lanes(i)
        tops = [top_v[d : d + 1, sl] for d in range(SLOTS)]
        top = functools.reduce(jnp.maximum, tops)
        shares = [jnp.exp2((t - top) * exp2_scale) for t in tops]
        norm = sum(shares[d] * norm_v[d : d + 1, sl] for d in range(SLOTS))
        inverse = 1.0 / norm
        weights = [share * inverse for share in shares]
        delta = jnp.zeros((1, TILE), f32)
        for d in range(SLOTS):
            at = pl.ds(d * tok, tok)
            pb = (s_v[at, sl] * weights[d]).astype(bf16)
            p_t[at, sl] = pb
            delta = delta + jnp.sum(pb.astype(f32) * dp_v[at, sl], axis=0, keepdims=True)
        for d in range(SLOTS):
            at = pl.ds(d * tok, tok)
            scaled = weights[d] * softmax_scale
            ds_t[at, sl] = (s_v[at, sl] * scaled * (dp_v[at, sl] - delta)).astype(bf16)

    def scores(first, count):
        def body(i, c):
            chunk(first, count, i)
            return c

        lax.fori_loop(0, tiles, body, 0, unroll=4)

    def last_scores(first, count):
        def body(i, c):
            chunk(first, count, i)
            finish(i)
            return c

        lax.fori_loop(0, tiles, body, 0, unroll=4)

    in_q.wait()
    lax.fori_loop(0, tiles, turn_q, 0, unroll=4)
    qr_f[...] = jnp.zeros_like(qr_f)
    in_qr.wait()
    for h in range(heads):
        qr_f[pl.ds(h, tok, stride=heads), :rope] = qr_ref[:, h * rope : (h + 1) * rope].astype(f32)
    lax.fori_loop(0, tiles, turn_rope, 0, unroll=4)
    lax.fori_loop(0, tiles, first_key, 0)
    unpack(0)
    in_do.wait()
    lax.fori_loop(0, tiles, turn_do, 0, unroll=4)
    after_z4()
    scores(0, 1)
    after_z2()
    unpack(2)
    scores(2, 1)
    core_copy(0, 0).wait_recv()
    unpack(1)
    scores(1, 1)
    after_y()
    unpack(4)
    scores(4, 1)
    core_copy(0, 1).wait_recv()
    unpack(3)
    last_scores(3, 1)

    def key_dots(first, count):
        at = pl.ds(first * tok, count * tok)
        g = jnp.dot(p_t[at, :], do_v[...], preferred_element_type=f32)
        g = g + jnp.dot(ds_t[at, :], q_v[...], preferred_element_type=f32)
        gr = jnp.dot(ds_t[at, :], qr_v[...], preferred_element_type=f32)
        for k in range(count):
            b = first + k + 1 - core
            piece = slice(k * tok, (k + 1) * tok)
            turned = gr[piece, :].T
            for q in range(QUARTERS):
                gbuf[b, q, :tok, :] = g[piece, q * LANES : (q + 1) * LANES].astype(bf16)
                gbuf[b, q, tok:, :] = turned[q * 16 : (q + 1) * 16, :].astype(bf16)

    def key_terms(first, count):
        key_dots(first, count)
        b_copy(first, count).start()

    def a1_copy(pair, k):
        two = pl.ds(2 * pair, 2)
        return remote(
            s1.at[other_y(k), two],
            ry.at[k - 1, two],
            a1s.at[pair, k - 1],
            a1r.at[pair, k - 1],
            at_y(k),
        )

    def a2_copy(pair, cross):
        n = pair - 1
        return remote(
            sz.at[n],
            rz.at[n, cross],
            a2s.at[n, cross],
            a2r.at[n, cross],
            along(-2 * pair, cross),
        )

    def a3_copy():
        return remote(sx, rx, a3s, a3r, px)

    def red1(pair):
        if pair == 0:
            b_copy(0, 1).wait_recv()
        elif pair == 1:
            b_copy(1, 2).wait_recv()
        else:
            b_copy(3, 2).wait_recv()
            b_unread().wait_recv()
        for b in (2 * pair, 2 * pair + 1):
            for q in range(QUARTERS):
                s1[q, b] = (gbuf[b, q, mine].astype(f32) + rc[b, q].astype(f32)).astype(bf16)
        for k in (2, 1, 3):
            a1_copy(pair, k).start()

    def red2(pair):
        two = pl.ds(2 * pair, 2)
        summed = s1[y, two].astype(f32)
        for k in (1, 2, 3):
            a1_copy(pair, k).wait_recv()
            summed = summed + ry[k - 1, two].astype(f32)
        if pair:
            sz[pair - 1] = summed.astype(bf16)
            a2_copy(pair, 1).start()
            a2_copy(pair, 0).start()
        else:
            sx[...] = summed.astype(bf16)
            a3_copy().start()

    def f_copy(cross, k):
        block = core if cross else 1 - core
        return remote(
            fo.at[block],
            obuf.at[y, core],
            fs.at[cross, k],
            fr.at[cross, k],
            at_y(k, sib) if cross else at_y(k),
        )

    def query_terms(i, c):
        sl = lanes(i)
        turned = jnp.dot(k_t[...], ds_t[:, sl], preferred_element_type=f32)
        dq_v[sl, :] = turned[:width, :].astype(bf16).T
        qr_f[sl, :rope] = turned[width:, :].T
        return c

    def query_run(first, last):
        lax.fori_loop(first, last, query_terms, 0)

    key_terms(3, 2)
    key_terms(1, 2)
    red1(2)
    key_terms(0, 1)
    red1(1)
    red1(0)
    query_run(0, 1)
    red2(2)
    red2(1)
    red2(0)
    query_run(1, 2)

    a3_copy().wait_recv()
    summed = sx[...].astype(f32) + rx[...].astype(f32)
    for pair in (2, 1):
        for cross in (0, 1):
            a2_copy(pair, cross).wait_recv()
        summed = summed + (rz[pair - 1, 0].astype(f32) + rz[pair - 1, 1].astype(f32))
    fo[...] = summed.astype(bf16)
    for k in (2, 1, 3):
        f_copy(0, k).start()
        f_copy(1, k).start()
    f_copy(1, 0).start()
    obuf[y, core] = fo[1 - core]
    query_run(2, tiles)
    for h in range(heads):
        dqr_ref[:, h * rope : (h + 1) * rope] = qr_f[pl.ds(h, tok, stride=heads), :rope].astype(bf16)
    for k in range(4):
        f_copy(1, k).wait_recv()
        if k:
            f_copy(0, k).wait_recv()
    for q in range(QUARTERS):
        sl = slice(q * LANES, (q + 1) * LANES)
        dlat_ref[:part, sl] = obuf[q, 0]
        dlat_ref[part:, sl] = obuf[q, 1, part - rest : tok - rest, :]
        drope_ref[q * 16 : (q + 1) * 16, :] = obuf[q, 1, tok - rest :, :]

    z2_copy().wait_send()
    z4_copy().wait_send()
    for n in range(2):
        core_copy(0, n).wait_send()
    b_copy(3, 2).wait_send()
    b_copy(1, 2).wait_send()
    b_copy(0, 1).wait_send()
    b_unread().wait_send()
    for k in (1, 2, 3):
        y_copy(k).wait_send()
        f_copy(0, k).wait_send()
        for pair in range(3):
            a1_copy(pair, k).wait_send()
    for n in range(4):
        f_copy(1, n).wait_send()
    for cross in (0, 1):
        a2_copy(1, cross).wait_send()
        a2_copy(2, cross).wait_send()
    a3_copy().wait_send()


def settle(*refs):
    half = (len(refs) - 1) // 2
    sems = refs[-1]
    copies = []
    for n in range(half):
        src, dst = refs[n], refs[half + n]
        pieces = 8 if n == 0 else 1
        step = src.shape[0] // pieces
        for p in range(pieces):
            at = pl.ds(p * step, step)
            copies.append(pltpu.make_async_copy(src.at[at], dst.at[at], sems.at[len(copies)]))
    for copy in copies:
        copy.start()
    for copy in copies:
        copy.wait()


def local(query_latent, query_rope, latent, rope_key, out_grad, doc_lengths, n_ctx):
    tok, heads, width = query_latent.shape
    rope = rope_key.shape[0]
    rows = tok * heads
    keys = SLOTS * tok
    krows = tok + rope * tok // width
    half = (krows // 2 + 15) // 16 * 16
    dma = pltpu.SemaphoreType.DMA
    vmem = pltpu.VMEM
    in_any = pl.BlockSpec(memory_space=pl.ANY)
    shapes = (
        jax.ShapeDtypeStruct((rows, width), bf16),
        jax.ShapeDtypeStruct((tok, heads * rope), bf16),
        jax.ShapeDtypeStruct((tok, width), bf16),
        jax.ShapeDtypeStruct((rope, tok), bf16),
    )
    outs = pl.pallas_call(
        functools.partial(kernel, n_ctx, heads),
        out_shape=tuple(vmem(x.shape, x.dtype) for x in shapes),
        in_specs=[pl.BlockSpec(memory_space=pltpu.SMEM), in_any, in_any, in_any, in_any, in_any],
        out_specs=(pl.BlockSpec(memory_space=pltpu.VMEM),) * 4,
        scratch_shapes=[
            vmem((tok, heads * rope), bf16),
            vmem((tok, width), bf16),
            vmem((rope, tok), bf16),
            vmem((rows, width), bf16),
            vmem((rows, width), bf16),
            vmem((width + LANES, rows), bf16),
            vmem((width, rows), bf16),
            vmem((rows, LANES), f32),
            vmem((rows, LANES), bf16),
            vmem((1, rows), jnp.int32),
            vmem((8, rows), f32),
            vmem((8, rows), f32),
            vmem((keys, rows), f32),
            vmem((keys, rows), f32),
            vmem((keys, rows), bf16),
            vmem((keys, rows), bf16),
            vmem((SLOTS, QUARTERS, krows, LANES), bf16),
            vmem((keys, width + LANES), bf16),
            vmem((width + rope, keys), bf16),
            vmem((BLOCKS, QUARTERS, krows, LANES), bf16),
            vmem((BLOCKS, QUARTERS, half, LANES), bf16),
            vmem((QUARTERS, BLOCKS, half, LANES), bf16),
            vmem((3, BLOCKS, half, LANES), bf16),
            vmem((2, 2, half, LANES), bf16),
            vmem((2, 2, 2, half, LANES), bf16),
            vmem((2, half, LANES), bf16),
            vmem((2, half, LANES), bf16),
            vmem((2, half, LANES), bf16),
            vmem((QUARTERS, 2, half, LANES), bf16),
            dma((5,)),
            dma((2,)),
            dma((2,)),
            dma((3,)),
            dma((3,)),
            dma((2,)),
            dma((2,)),
            dma((4,)),
            dma((4,)),
            dma((3, 3)),
            dma((3, 3)),
            dma((2, 2)),
            dma((2, 2)),
            dma,
            dma,
            dma((2, 4)),
            dma((2, 4)),
        ],
        compiler_params=pltpu.CompilerParams(
            collective_id=0, has_side_effects=True, vmem_limit_bytes=56 * 1024 * 1024
        ),
    )(
        doc_lengths,
        query_latent.reshape(rows, width),
        out_grad.reshape(rows, width),
        query_rope,
        latent,
        rope_key,
    )
    dq, dqr, dlat, drope = pl.pallas_call(
        settle,
        out_shape=shapes,
        in_specs=[in_any] * 4,
        out_specs=(in_any,) * 4,
        scratch_shapes=[dma((11,))],
        compiler_params=pltpu.CompilerParams(vmem_limit_bytes=1024 * 1024),
    )(*outs)
    return dq.reshape(tok, heads, width), dqr, dlat, drope


def solution(mesh):
    in_specs = (
        P("ctx", "head", None),
        P("ctx", "head"),
        P("ctx", None),
        P(None, "ctx"),
        P("ctx", "head", None),
        P(),
    )
    out_specs = (P("ctx", "head", None), P("ctx", "head"), P("ctx", None), P(None, "ctx"))
    return jax.shard_map(
        functools.partial(local, n_ctx=mesh.shape["ctx"]),
        mesh=mesh,
        in_specs=in_specs,
        out_specs=out_specs,
        check_vma=False,
    )
```
